32 devices in a mesh: dp: 4 (over y, x), gx: 4 (over z), gy: 2 (over core).
Axes of the slice: x: 2, y: 2, z: 4, core: 2. Of those that a mesh axis runs over, the one named last changes fastest.
Arguments:
- hidden_in: bfloat16 [4, 1024, 768], P('dp', 'gx', 'gy'), may hold values from -6 to 6
- encoded: bfloat16 [4, 1024, 768], P('dp', 'gx', 'gy'), may hold values from -6 to 6
- doc_ids: int32 [4, 1024], P('dp'), may hold values from 0 to 7, never falling along the last dimension, each value on 1 to 768 neighbouring positions
- buckets: int32 [1024], replicated, may hold values from 0 to 31, as said below
- rel_table: float32 [32, 12], replicated, may hold values from -6 to 6
- norm_gains: float32 [3, 768], replicated, may hold values from 0.5 to 1.5
- self_q: bfloat16 [768, 768], P('gy', 'gx'), may hold values from -0.02734375 to 0.02734375
- self_k: bfloat16 [768, 768], P('gy', 'gx'), may hold values from -0.21875 to 0.21875
- self_v: bfloat16 [768, 768], P('gy', 'gx'), may hold values from -0.21875 to 0.21875
- self_out: bfloat16 [768, 768], P('gx', 'gy'), may hold values from -1.75 to 1.75
- cross_q: bfloat16 [768, 768], P('gy', 'gx'), may hold values from -0.02734375 to 0.02734375
- cross_k: bfloat16 [768, 768], P('gy', 'gx'), may hold values from -0.21875 to 0.21875
- cross_v: bfloat16 [768, 768], P('gy', 'gx'), may hold values from -0.21875 to 0.21875
- cross_out: bfloat16 [768, 768], P('gx', 'gy'), may hold values from -3.5 to 3.5
- ff_gate: bfloat16 [768, 2048], P('gy', 'gx'), may hold values from -0.21875 to 0.21875
- ff_up: bfloat16 [768, 2048], P('gy', 'gx'), may hold values from -0.21875 to 0.21875
- ff_down: bfloat16 [2048, 768], P('gx', 'gy'), may hold values from -0.125 to 0.125
- grad_out: bfloat16 [4, 1024, 768], P('dp', 'gx', 'gy'), may hold values from -6 to 6
Outputs:
- layer_out: bfloat16 [4, 1024, 768], P('dp', 'gx', 'gy')
- grad_hidden: float32 [4, 1024, 768], P('dp', 'gx', 'gy')
- grad_encoded: float32 [4, 1024, 768], P('dp', 'gx', 'gy')
- grad_gains: float32 [3, 768], replicated
- grad_rel: float32 [32, 12], replicated
- grad_self_q: float32 [768, 768], P('gy', 'gx')
- grad_self_k: float32 [768, 768], P('gy', 'gx')
- grad_self_v: float32 [768, 768], P('gy', 'gx')
- grad_self_out: float32 [768, 768], P('gx', 'gy')
- grad_cross_q: float32 [768, 768], P('gy', 'gx')
- grad_cross_k: float32 [768, 768], P('gy', 'gx')
- grad_cross_v: float32 [768, 768], P('gy', 'gx')
- grad_cross_out: float32 [768, 768], P('gx', 'gy')
- grad_ff_gate: float32 [768, 2048], P('gy', 'gx')
- up_projection_gradient: float32 [768, 2048], P('gy', 'gx')
- grad_ff_down: float32 [2048, 768], P('gx', 'gy')
The draws below stay inside these ranges and needn't reach their ends.
Inputs may be any that keep to these rules, and one draw needn't show every extreme that they name: `buckets`: nondecreasing in the distance, 0 at distance 0 and 31 at distance 1024 - 1. `doc_ids`: document numbers never fall along a sequence; each of the 8 documents has 1 to 768 tokens and one has exactly that many.
All inputs are finite; a program needn't handle non-finite values.
Results may differ from the reference program's by a relative error of at most 0.023.
Values may be sent and summed in bfloat16 or wider, within the bound.
A program may use at most 128 MiB of HBM per device.

```python
import math
import jax
import jax.numpy as jnp
import numpy as np
from jax import lax

D = 768
H = 12
DH = 64
FF = 2048
NB = 32
SEQ = 1024
ENC = 1024
DOCS = 8
SEQS = 4


def draw_buckets(key, part):
    key = jax.random.fold_in(key, 11)
    offsets = jnp.arange(SEQ, dtype=jnp.int32)
    tosses = jax.random.randint(key, (SEQ,), 0, SEQ)
    climbs = (tosses < 8 * SEQ // (offsets + 8)).astype(jnp.int32)
    climbs = jnp.where(offsets == 0, 0, jnp.where(offsets == 1, 1, climbs))
    running = jnp.cumsum(climbs)
    return (running * (NB - 1) // running[-1]).astype(jnp.int32)


def level_of(key, dims, cuts, low, high):
    def one(axis_at, shards_of):
        heights = jax.random.uniform(jax.random.fold_in(jax.random.fold_in(key, 6), axis_at), (shards_of,), jnp.float32, low / len(cuts), high / len(cuts))
        return jnp.repeat(jnp.exp(heights), dims[axis_at] // shards_of).reshape((-1,) + (1,) * (len(dims) - axis_at - 1))

    level = one(*cuts[0])
    for cut in cuts[1:]:
        level = level * one(*cut)
    return level


def profile(count, total, limit, slope):
    weights = [(1 << 20) // math.isqrt(standing ** slope) + 1 for standing in range(2, count + 1)]
    spare, counts = total - limit - (count - 1), [1] * (count - 1)
    while spare > 0:
        candidates = [i for i in range(count - 1) if counts[i] < limit]
        whole, remaining = sum([weights[i] for i in candidates]), spare
        for i in candidates:
            extra = min(limit - counts[i], max(1, remaining * weights[i] // whole), spare)
            counts[i] = counts[i] + extra
            spare = spare - extra
    return np.array([limit] + counts)


def uneven_parts(own_key, amount, total, reach, slope):
    if amount == 2:
        one = jax.random.randint(own_key, (), max(1, total - reach), min(reach, total - 1) + 1)
        return jnp.stack([one, total - one])
    lengths = jnp.asarray(profile(amount, total, reach, slope), jnp.int32)
    twos = (amount - 1) // 2
    source_of, taker = lengths[1:1 + 2 * twos:2], lengths[2:2 + 2 * twos:2]
    room = jnp.minimum(source_of - 1, reach - taker)
    passed = jax.random.randint(jax.random.fold_in(own_key, 1), (twos,), 0, 1 << 20) % (room + 1)
    lengths = lengths.at[1:1 + 2 * twos:2].set(source_of - passed).at[2:2 + 2 * twos:2].set(taker + passed)
    return lengths[jax.random.permutation(jax.random.fold_in(own_key, 2), amount)]


def gaussian(key, extent, scale, reach, split=(), kind=jnp.bfloat16):
    array = scale * jax.random.normal(key, extent, jnp.float32)
    if split:
        array = array * level_of(key, extent, split, -0.22, 0.18)
    return jnp.clip(array, -reach, reach).astype(kind)


def setup_inputs(seed: int = 0) -> dict:
    key_of = jax.random.split(jax.random.key(seed), 19)
    return {
        "hidden_in": gaussian(key_of[0], (SEQS, SEQ, D), 1.0, 6.0, ((0, 4), (1, 4), (2, 2))),
        "encoded": gaussian(key_of[1], (SEQS, ENC, D), 1.0, 6.0, ((0, 4), (1, 4), (2, 2))),
        "doc_ids": jax.vmap(lambda own: jnp.searchsorted(jnp.cumsum(uneven_parts(own, DOCS, SEQ, 3 * SEQ // 4, 0)), jnp.arange(SEQ), side="right"))(jax.random.split(key_of[2], SEQS)).reshape((SEQS, SEQ)).astype(jnp.int32),
        "buckets": draw_buckets(jax.random.fold_in(key_of[18], 71), 0),
        "rel_table": gaussian(key_of[4], (NB, H), 1.0, 6.0, (), jnp.float32),
        "norm_gains": jnp.clip(1.0 + 0.1 * jax.random.normal(key_of[5], (3, D), jnp.float32), 0.5, 1.5),
        "self_q": gaussian(key_of[6], (D, H * DH), (D * DH) ** -0.5, 0.02734375, ((0, 2), (1, 4))),
        "self_k": gaussian(key_of[7], (D, H * DH), D ** -0.5, 0.21875, ((0, 2), (1, 4))),
        "self_v": gaussian(key_of[8], (D, H * DH), D ** -0.5, 0.21875, ((0, 2), (1, 4))),
        "self_out": gaussian(key_of[9], (H * DH, D), (H * DH * 16 // SEQ) ** -0.5, 1.75, ((0, 4), (1, 2))),
        "cross_q": gaussian(key_of[10], (D, H * DH), (D * DH) ** -0.5, 0.02734375, ((0, 2), (1, 4))),
        "cross_k": gaussian(key_of[11], (D, H * DH), D ** -0.5, 0.21875, ((0, 2), (1, 4))),
        "cross_v": gaussian(key_of[12], (D, H * DH), D ** -0.5, 0.21875, ((0, 2), (1, 4))),
        "cross_out": gaussian(key_of[13], (H * DH, D), (H * DH * 4 // ENC) ** -0.5, 3.5, ((0, 4), (1, 2))),
        "ff_gate": gaussian(key_of[14], (D, FF), D ** -0.5, 0.21875, ((0, 2), (1, 4))),
        "ff_up": gaussian(key_of[15], (D, FF), D ** -0.5, 0.21875, ((0, 2), (1, 4))),
        "ff_down": gaussian(key_of[16], (FF, D), FF ** -0.5, 0.125, ((0, 4), (1, 2))),
        "grad_out": gaussian(key_of[17], (SEQS, SEQ, D), 1.0, 6.0, ((0, 4), (1, 4), (2, 2))),
    }


epsilon = 1e-06
masked_score = -1000000000.0
highest = lax.Precision.HIGHEST

@jax.custom_vjp
def low(v):
    return lax.optimization_barrier(v.astype(jnp.bfloat16)).astype(jnp.float32)

@jax.custom_vjp
def low_back(v):
    return v

def low_keep(v):
    return (low(v), None)

def low_pass(kept, grad):
    return (grad,)

def back_keep(v):
    return (v, None)

def back_low(kept, grad):
    return (low(grad),)
low.defvjp(low_keep, low_pass)
low_back.defvjp(back_keep, back_low)

def rms_norm(stream, gain):
    return stream * lax.rsqrt(lax.optimization_barrier(jnp.mean(stream * stream, axis=-1, keepdims=True)) + epsilon) * gain

def matmul(left, right):
    return jnp.dot(left, right, precision=highest)

def attention(queries, key_rows, value_rows, bias, allowed):
    query_heads = queries.reshape(queries.shape[0], -1, DH)
    key_heads = key_rows.reshape(key_rows.shape[0], -1, DH)
    value_heads = value_rows.reshape(value_rows.shape[0], -1, DH)
    scores = jnp.einsum('qhd,khd->hqk', query_heads, key_heads, precision=highest)
    if bias is not None:
        scores = scores + bias
    scores = low_back(scores)
    if allowed is not None:
        scores = jnp.where(allowed[None], scores, masked_score)
    row_top = lax.optimization_barrier(jnp.max(scores, axis=-1, keepdims=True))
    exponent = jnp.exp(scores - row_top)
    chances = low(exponent / lax.optimization_barrier(jnp.sum(exponent, axis=-1, keepdims=True)))
    context = jnp.einsum('hqk,khd->qhd', chances, value_heads, precision=highest)
    return low_back(low(context.reshape(queries.shape)))

def layer(stream, enc_rows, docs, buckets, rel_table, gains, self_q, self_k, self_v, self_out, cross_q, cross_k, cross_v, cross_out, ff_gate, ff_up, ff_down):
    positions = jnp.arange(SEQ, dtype=jnp.int32)
    normed_one = low(rms_norm(stream, gains[0]))
    queries = low_back(low(matmul(normed_one, self_q)))
    key_rows = low_back(low(matmul(normed_one, self_k)))
    value_rows = low_back(low(matmul(normed_one, self_v)))
    distance = jnp.clip(positions[:, None] - positions[None, :], 0, SEQ - 1)
    bias = jnp.transpose(rel_table[buckets[distance]], (2, 0, 1))
    allowed = (positions[None, :] <= positions[:, None]) & (docs[:, None] == docs[None, :])
    context = attention(queries, key_rows, value_rows, bias, allowed)
    stream_one = stream + low_back(matmul(context, self_out))
    normed_two = low(rms_norm(stream_one, gains[1]))
    cross_queries = low_back(low(matmul(normed_two, cross_q)))
    cross_keys = low_back(low(matmul(enc_rows, cross_k)))
    cross_values = low_back(low(matmul(enc_rows, cross_v)))
    cross_context = attention(cross_queries, cross_keys, cross_values, None, None)
    stream_two = stream_one + low_back(matmul(cross_context, cross_out))
    normed_three = low(rms_norm(stream_two, gains[2]))
    gate = low_back(matmul(normed_three, ff_gate))
    up_part = low_back(matmul(normed_three, ff_up))
    hidden = low(jax.nn.gelu(gate, approximate=True) * up_part)
    return stream_two + low_back(matmul(hidden, ff_down))

def reference(hidden_in, encoded, doc_ids, buckets, rel_table, norm_gains, self_q, self_k, self_v, self_out, cross_q, cross_k, cross_v, cross_out, ff_gate, ff_up, ff_down, grad_out):
    weight_list = tuple((w.astype(jnp.float32) for w in (self_q, self_k, self_v, self_out, cross_q, cross_k, cross_v, cross_out, ff_gate, ff_up, ff_down)))
    params = (rel_table.astype(jnp.float32), norm_gains.astype(jnp.float32)) + weight_list

    def one_sequence(carry, members):
        stream, enc_rows, docs, cotangent = members

        def forward(stream, enc_rows, *rest):
            return layer(stream, enc_rows, docs, buckets, *rest)
        result, pullback = jax.vjp(forward, stream, enc_rows, *params)
        grads = pullback(cotangent)
        updated = tuple((a + b for a, b in zip(carry, grads[2:])))
        return (updated, (result.astype(jnp.bfloat16), grads[0], grads[1]))
    initial = tuple((jnp.zeros(p.shape, jnp.float32) for p in params))
    reduced_total, (layer_out, grad_hidden, grad_encoded) = lax.scan(one_sequence, initial, (hidden_in.astype(jnp.float32), encoded.astype(jnp.float32), doc_ids, grad_out.astype(jnp.float32)))
    return (layer_out, grad_hidden, grad_encoded, reduced_total[1], reduced_total[0], reduced_total[2], reduced_total[3], reduced_total[4], reduced_total[5], reduced_total[6], reduced_total[7], reduced_total[8], reduced_total[9], reduced_total[10], reduced_total[11], reduced_total[12])
```

```python
import functools

import jax
import jax.numpy as jnp
from jax import lax
from jax.experimental import pallas as pl
from jax.experimental.pallas import tpu as pltpu
from jax.sharding import PartitionSpec as P

DH = 64
epsilon = 1e-06
masked_score = -1000000000.0
f32 = jnp.float32
bf16 = jnp.bfloat16
VMEM_LIMIT = 48 * 1024 * 1024


def mm(a, b):
    return jnp.dot(a, b, preferred_element_type=f32)


def mm_t(a, b):
    return lax.dot_general(a, b, (((1,), (1,)), ((), ())), preferred_element_type=f32)


def t_mm(a, b):
    return lax.dot_general(a, b, (((0,), (0,)), ((), ())), preferred_element_type=f32)


def gather_tokens(own):
    return lax.all_gather(own, "gx", axis=0, tiled=True)


def scatter_tokens(partial_sums):
    return lax.psum_scatter(
        partial_sums.astype(bf16), "gx", scatter_dimension=0, tiled=True
    ).astype(f32)


def swap(value):
    size = lax.axis_size("gy")
    return lax.ppermute(value, "gy", [(i, size - 1 - i) for i in range(size)])


def natural_rows(pair_ref, width, start, block):
    pieces = []
    for b in range(2 * (width // (2 * block))):
        pieces.append(pair_ref[b % 2, (b // 2) * block : (b // 2 + 1) * block, start : start + DH])
    return jnp.concatenate(pieces, axis=0)


def softmax_rows(scores):
    top = jnp.max(scores, axis=-1, keepdims=True)
    e = jnp.exp(scores - top)
    return e * (1.0 / jnp.sum(e, axis=-1, keepdims=True))


def bias_tile(vec_ref, head, block):
    row = vec_ref[head : head + 1, :]
    return pltpu.roll(
        jnp.broadcast_to(row, (block, row.shape[1])), 0, 1, stride=1, stride_axis=0
    )


def rotate_lanes(x, amount):
    if amount == 0:
        return x
    width = x.shape[1]
    return jnp.concatenate([x[:, width - amount :], x[:, : width - amount]], axis=1)


def self_mask(core_ref, dq_ref, dk_ref, g, width, block):
    first = (2 * g + core_ref[0]) * block
    rows = first + lax.broadcasted_iota(jnp.int32, (block, width), 0)
    cols = lax.broadcasted_iota(jnp.int32, (block, width), 1)
    own = dq_ref[g * block : (g + 1) * block, :]
    return (cols <= rows) & (own == dk_ref[:, :width])


def self_scores(q, k, tile, mask, g, width, block):
    return jnp.where(mask, mm_t(q, k) + rotate_lanes(tile, 2 * block * g)[:, :width], masked_score)


def self_forward_kernel(block, heads, core_ref, q_ref, kv_ref, dq_ref, dk_ref, vec_ref, out_ref):
    groups = q_ref.shape[0] // block
    keys = 2 * q_ref.shape[0]
    masks = [
        self_mask(core_ref, dq_ref, dk_ref, g, 2 * block * (g + 1), block) for g in range(groups)
    ]
    parts = [[] for _ in range(groups)]
    for h in range(heads):
        k = natural_rows(kv_ref, keys, h * DH, block)
        v = natural_rows(kv_ref, keys, (heads + h) * DH, block)
        tile = bias_tile(vec_ref, h, block)
        for g in range(groups):
            width = 2 * block * (g + 1)
            q = q_ref[g * block : (g + 1) * block, h * DH : (h + 1) * DH]
            p = softmax_rows(self_scores(q, k[:width], tile, masks[g], g, width, block))
            parts[g].append(mm(p.astype(bf16), v[:width]))
    for g in range(groups):
        out_ref[g * block : (g + 1) * block, :] = jnp.concatenate(parts[g], axis=1).astype(bf16)


def self_backward_kernel(
    block, heads, core_ref, q_ref, kv_ref, dq_ref, dk_ref, vec_ref, dc_ref, gq_ref, gkv_ref, gd_ref
):
    groups = q_ref.shape[0] // block
    keys = 2 * q_ref.shape[0]
    masks = [
        self_mask(core_ref, dq_ref, dk_ref, g, 2 * block * (g + 1), block) for g in range(groups)
    ]
    flip = (
        lax.broadcasted_iota(jnp.int32, (block, block), 0)
        + lax.broadcasted_iota(jnp.int32, (block, block), 1)
        == block - 1
    ).astype(bf16)
    parts = [[] for _ in range(groups)]
    gd_ref[...] = jnp.zeros_like(gd_ref)
    for h in range(heads):
        k = natural_rows(kv_ref, keys, h * DH, block)
        v = natural_rows(kv_ref, keys, (heads + h) * DH, block)
        tile = bias_tile(vec_ref, h, block)
        gk_total = None
        gv_total = None
        shifted = None
        for g in range(groups - 1, -1, -1):
            width = 2 * block * (g + 1)
            q = q_ref[g * block : (g + 1) * block, h * DH : (h + 1) * DH]
            dc = dc_ref[g * block : (g + 1) * block, h * DH : (h + 1) * DH]
            p = softmax_rows(self_scores(q, k[:width], tile, masks[g], g, width, block))
            dp = mm_t(dc, v[:width])
            inner = jnp.sum(dp * p, axis=-1, keepdims=True)
            ds = (p * (dp - inner)).astype(bf16)
            parts[g].append(mm(ds, k[:width]))
            gk = t_mm(q, ds)
            gv = t_mm(dc, p.astype(bf16))
            flipped = mm(flip, ds)
            if gk_total is None:
                gk_total, gv_total = gk, gv
                shifted = rotate_lanes(flipped, keys - 2 * block * g) if g else flipped
            else:
                rest = jnp.zeros((DH, keys - width), f32)
                gk_total = gk_total + jnp.concatenate([gk, rest], axis=1)
                gv_total = gv_total + jnp.concatenate([gv, rest], axis=1)
                flipped = jnp.concatenate(
                    [flipped, jnp.zeros((block, keys - width), f32)], axis=1
                )
                if g:
                    flipped = rotate_lanes(flipped, keys - 2 * block * g)
                shifted = shifted + flipped
        for b in range(2 * groups):
            lanes = slice((b // 2) * block, (b // 2 + 1) * block)
            source = slice(b * block, (b + 1) * block)
            gkv_ref[b % 2, h * DH : (h + 1) * DH, lanes] = gk_total[:, source].astype(bf16)
            gkv_ref[b % 2, (heads + h) * DH : (heads + h + 1) * DH, lanes] = gv_total[
                :, source
            ].astype(bf16)
        gd_ref[h : h + 1, :] = jnp.sum(
            pltpu.roll(shifted, 0, 1, stride=1, stride_axis=0), axis=0, keepdims=True
        )
    for g in range(groups):
        gq_ref[g * block : (g + 1) * block, :] = jnp.concatenate(parts[g], axis=1).astype(bf16)


def cross_forward_kernel(block, heads, q_ref, kv_ref, out_ref):
    rows = q_ref.shape[0]
    for h in range(heads):
        k = jnp.concatenate([kv_ref[c, :, h * DH : (h + 1) * DH] for c in range(2)], axis=0)
        v = jnp.concatenate(
            [kv_ref[c, :, (heads + h) * DH : (heads + h + 1) * DH] for c in range(2)], axis=0
        )
        for r in range(0, rows, block):
            p = softmax_rows(mm_t(q_ref[r : r + block, h * DH : (h + 1) * DH], k))
            out_ref[r : r + block, h * DH : (h + 1) * DH] = mm(p.astype(bf16), v).astype(bf16)


def cross_backward_kernel(block, heads, q_ref, kv_ref, dc_ref, gq_ref, gkv_ref):
    rows = q_ref.shape[0]
    for h in range(heads):
        k = jnp.concatenate([kv_ref[c, :, h * DH : (h + 1) * DH] for c in range(2)], axis=0)
        v = jnp.concatenate(
            [kv_ref[c, :, (heads + h) * DH : (heads + h + 1) * DH] for c in range(2)], axis=0
        )
        gk_total = None
        for r in range(0, rows, block):
            q = q_ref[r : r + block, h * DH : (h + 1) * DH]
            dc = dc_ref[r : r + block, h * DH : (h + 1) * DH]
            p = softmax_rows(mm_t(q, k))
            dp = mm_t(dc, v)
            inner = jnp.sum(dp * p, axis=-1, keepdims=True)
            ds = (p * (dp - inner)).astype(bf16)
            gq_ref[r : r + block, h * DH : (h + 1) * DH] = mm(ds, k).astype(bf16)
            gk = t_mm(q, ds)
            gv = t_mm(dc, p.astype(bf16))
            gk_total = gk if gk_total is None else gk_total + gk
            gv_total = gv if r == 0 else gv_total + gv
        for c in range(2):
            source = slice(c * rows, (c + 1) * rows)
            gkv_ref[c, h * DH : (h + 1) * DH, :] = gk_total[:, source].astype(bf16)
            gkv_ref[c, (heads + h) * DH : (heads + h + 1) * DH, :] = gv_total[:, source].astype(
                bf16
            )


def call(kernel, out_shape, smem, name):
    vm = pl.BlockSpec(memory_space=pltpu.VMEM)

    def run(*operands):
        specs = [pl.BlockSpec(memory_space=pltpu.SMEM)] * smem + [vm] * (len(operands) - smem)
        multi = isinstance(out_shape, (list, tuple))
        return pl.pallas_call(
            kernel,
            out_shape=out_shape,
            in_specs=specs,
            out_specs=[vm] * len(out_shape) if multi else vm,
            compiler_params=pltpu.CompilerParams(vmem_limit_bytes=VMEM_LIMIT),
            name=name,
        )(*operands)

    return run


def norm_forward(stream, gain):
    root = lax.rsqrt(jnp.mean(stream * stream, axis=-1, keepdims=True) + epsilon)
    plain = stream * root
    return (plain * gain).astype(bf16), plain, root


def norm_backward(dy, plain, root, gain):
    scaled = dy * gain
    inner = jnp.mean(scaled * plain, axis=-1, keepdims=True)
    return root * (scaled - plain * inner), jnp.sum(dy * plain, axis=0)


def glu_piece(gate, up_part):
    return jax.nn.gelu(gate, approximate=True) * up_part


def body(
    hidden_in,
    encoded,
    doc_ids,
    buckets,
    rel_table,
    norm_gains,
    self_q,
    self_k,
    self_v,
    self_out,
    cross_q,
    cross_k,
    cross_v,
    cross_out,
    ff_gate,
    ff_up,
    ff_down,
    grad_out,
):
    core = lax.axis_index("gy")
    column = lax.axis_index("gx")
    groups = lax.axis_size("gx")
    seq_len = doc_ids.shape[1]
    half = hidden_in.shape[2]
    block = hidden_in.shape[1] // 2
    proj = self_q.shape[1]
    heads = proj // DH
    hid_part = ff_gate.shape[1]
    own_tokens = groups * block
    core_one = core.reshape(1).astype(jnp.int32)

    def to_rows(x):
        return lax.all_to_all(x, "gy", x.ndim - 2, x.ndim - 1, tiled=True)

    def to_features(x):
        return lax.all_to_all(x, "gy", x.ndim - 1, x.ndim - 2, tiled=True)

    first_rows = to_rows(hidden_in[0])
    w_self = lax.all_gather(
        jnp.concatenate([self_q, self_k, self_v], axis=1), "gy", axis=0, tiled=True
    )
    both_rows = to_rows(jnp.concatenate([encoded, grad_out], axis=0))
    w_cross = lax.all_gather(
        jnp.concatenate([cross_q, cross_k, cross_v], axis=1), "gy", axis=0, tiled=True
    )
    w_ff = lax.all_gather(jnp.concatenate([ff_gate, ff_up], axis=1), "gy", axis=0, tiled=True)
    w_outs = lax.all_gather(
        jnp.concatenate([self_out, cross_out, ff_down], axis=0), "gy", axis=1, tiled=True
    )
    w_self_out, w_cross_out, w_down = (
        w_outs[:proj],
        w_outs[proj : 2 * proj],
        w_outs[2 * proj :],
    )
    w_cq, w_ckv = w_cross[:, :proj], w_cross[:, proj:]

    distance_from = (core * block - jnp.arange(seq_len, dtype=jnp.int32)) % seq_len
    table_part = lax.dynamic_slice_in_dim(rel_table, column * heads, heads, 1)

    def hot(distances):
        return (
            buckets[distances][None, :]
            == jnp.arange(rel_table.shape[0], dtype=jnp.int32)[:, None]
        ).astype(f32)

    bias_vec = lax.dot_general(
        table_part,
        hot(distance_from),
        (((0,), (0,)), ((), ())),
        precision=lax.Precision.HIGHEST,
    )
    docs_k = doc_ids
    docs_q = lax.dynamic_index_in_dim(
        doc_ids.reshape(groups, 2, block), core, 1, keepdims=False
    ).reshape(own_tokens, 1)

    stream0 = first_rows.astype(f32)
    low_one, plain_one, root_one = norm_forward(stream0, norm_gains[0])
    rows_one = gather_tokens(low_one)
    qkv = mm(rows_one, w_self).astype(bf16)
    q1 = qkv[:, :proj]
    kv1 = lax.all_gather(qkv[:, proj:], "gy", axis=0)

    enc_rows = gather_tokens(both_rows[0])
    kv2_own = mm(enc_rows, w_ckv).astype(bf16)
    kv2 = lax.all_gather(kv2_own, "gy", axis=0)
    out_rows = gather_tokens(both_rows[1])
    d_hid = mm_t(out_rows, w_down)

    ctx1 = call(
        functools.partial(self_forward_kernel, block, heads),
        jax.ShapeDtypeStruct((own_tokens, proj), bf16),
        1,
        "self_forward",
    )(core_one, q1, kv1, docs_q, docs_k, bias_vec)
    stream1 = stream0 + scatter_tokens(mm(ctx1, w_self_out))
    low_two, plain_two, root_two = norm_forward(stream1, norm_gains[1])
    rows_two = gather_tokens(low_two)
    q2 = mm(rows_two, w_cq).astype(bf16)
    ctx2 = call(
        functools.partial(cross_forward_kernel, 2 * block, heads),
        jax.ShapeDtypeStruct((own_tokens, proj), bf16),
        0,
        "cross_forward",
    )(q2, kv2)
    stream2 = stream1 + scatter_tokens(mm(ctx2, w_cross_out))
    low_three, plain_three, root_three = norm_forward(stream2, norm_gains[2])
    rows_three = gather_tokens(low_three)
    gate_up = mm(rows_three, w_ff)
    hidden_float, glu_pull = jax.vjp(glu_piece, gate_up[:, :hid_part], gate_up[:, hid_part:])
    hid = hidden_float.astype(bf16)
    d_gate, d_up = glu_pull(d_hid)
    d_gu = jnp.concatenate([d_gate, d_up], axis=1).astype(bf16)

    def own_half(x, which):
        return lax.dynamic_slice_in_dim(x, which * half, half, 1)

    def grad_cols(rows, d):
        other = t_mm(own_half(rows, 1 - core), d).astype(bf16)
        return t_mm(own_half(rows, core), d) + swap(other).astype(f32)

    def grad_rows(left, rows):
        other = t_mm(left, own_half(rows, 1 - core)).astype(bf16)
        return t_mm(left, own_half(rows, core)) + swap(other).astype(f32)

    def over_sequences(value):
        return lax.psum(value.astype(bf16), "dp")

    back_partial = mm_t(d_gu, w_ff)
    dn3 = scatter_tokens(back_partial)
    layer_rows = (stream2 + scatter_tokens(mm(hid, w_down))).astype(bf16)
    layer_out = to_features(layer_rows)[None]
    g_gu = grad_cols(rows_three, d_gu)
    g_down = grad_rows(hid, out_rows)
    back_three, gain_three = norm_backward(dn3, plain_three, root_three, norm_gains[2])
    g2 = both_rows[1].astype(f32) + back_three
    rows_a2 = gather_tokens(g2.astype(bf16))
    dctx2 = mm_t(rows_a2, w_cross_out).astype(bf16)
    dq2, dkv2_both = call(
        functools.partial(cross_backward_kernel, 2 * block, heads),
        (
            jax.ShapeDtypeStruct((own_tokens, proj), bf16),
            jax.ShapeDtypeStruct((2, 2 * proj, own_tokens), bf16),
        ),
        0,
        "cross_backward",
    )(q2, kv2, dctx2)

    def pair_sum(both):
        other = lax.dynamic_index_in_dim(both, 1 - core, 0, keepdims=False)
        own = lax.dynamic_index_in_dim(both, core, 0, keepdims=False)
        return (own.astype(f32) + swap(other).astype(f32)).astype(bf16)

    dn2 = scatter_tokens(mm_t(dq2, w_cq))
    dkv2 = pair_sum(dkv2_both)
    back_two, gain_two = norm_backward(dn2, plain_two, root_two, norm_gains[1])
    g1 = g2 + back_two
    rows_a1 = gather_tokens(g1.astype(bf16))
    dctx1 = mm_t(rows_a1, w_self_out).astype(bf16)
    grad_encoded = to_features(
        scatter_tokens(lax.dot_general(dkv2, w_ckv, (((0,), (1,)), ((), ())), preferred_element_type=f32))
    )[None]
    g_cq = grad_cols(rows_two, dq2)

    def grad_cols_t(rows, d_t):
        other = mm(d_t, own_half(rows, 1 - core)).astype(bf16)
        return (mm(d_t, own_half(rows, core)) + swap(other).astype(f32)).T

    g_ckv = grad_cols_t(enc_rows, dkv2)
    g_cross_out = grad_rows(ctx2, rows_a2)

    dq1, dkv1_both, by_shift = call(
        functools.partial(self_backward_kernel, block, heads),
        (
            jax.ShapeDtypeStruct((own_tokens, proj), bf16),
            jax.ShapeDtypeStruct((2, 2 * proj, own_tokens), bf16),
            jax.ShapeDtypeStruct((8, seq_len), f32),
        ),
        1,
        "self_backward",
    )(core_one, q1, kv1, docs_q, docs_k, bias_vec, dctx1)
    dkv1 = pair_sum(dkv1_both)
    dn1 = scatter_tokens(
        mm_t(dq1, w_self[:, :proj])
        + lax.dot_general(dkv1, w_self[:, proj:], (((0,), (1,)), ((), ())), preferred_element_type=f32)
    )
    back_one, gain_one = norm_backward(dn1, plain_one, root_one, norm_gains[0])
    grad_hidden = to_features(g1 + back_one)[None]
    g_q = grad_cols(rows_one, dq1)
    g_kv = grad_cols_t(rows_one, dkv1)
    g_self_out = grad_rows(ctx1, rows_a1)

    shift_distance = (
        core * block + block - 1 - jnp.arange(seq_len, dtype=jnp.int32)
    ) % seq_len
    table_grad = lax.dot_general(
        hot(shift_distance),
        by_shift[:heads],
        (((1,), (1,)), ((), ())),
        precision=lax.Precision.HIGHEST,
    )
    rel_full = lax.dynamic_update_slice(
        jnp.zeros(rel_table.shape, f32), table_grad, (0, column * heads)
    )
    gains = jnp.stack([gain_one, gain_two, gain_three])
    grad_gains, grad_rel = lax.psum((gains, rel_full), ("dp", "gx", "gy"))

    ff_flat = jnp.concatenate([g_gu.reshape(-1), g_down.reshape(-1)])
    ff_sum = over_sequences(ff_flat).astype(f32)
    cut = g_gu.size
    s_gu = ff_sum[:cut].reshape(g_gu.shape)
    s_down = ff_sum[cut:].reshape(g_down.shape)
    s_cross = over_sequences(jnp.concatenate([g_cq, g_ckv], axis=1)).astype(f32)
    s_cross_out = over_sequences(g_cross_out).astype(f32)
    s_self = over_sequences(jnp.concatenate([g_q, g_kv], axis=1)).astype(f32)
    s_self_out = over_sequences(g_self_out).astype(f32)
    return (
        layer_out,
        grad_hidden,
        grad_encoded,
        grad_gains,
        grad_rel,
        s_self[:, :proj],
        s_self[:, proj : 2 * proj],
        s_self[:, 2 * proj :],
        s_self_out,
        s_cross[:, :proj],
        s_cross[:, proj : 2 * proj],
        s_cross[:, 2 * proj :],
        s_cross_out,
        s_gu[:, :hid_part],
        s_gu[:, hid_part:],
        s_down,
    )


def solution(mesh):
    placed = (
        P("dp", "gx", "gy"),
        P("dp", "gx", "gy"),
        P("dp", None),
        P(),
        P(),
        P(),
        P("gy", "gx"),
        P("gy", "gx"),
        P("gy", "gx"),
        P("gx", "gy"),
        P("gy", "gx"),
        P("gy", "gx"),
        P("gy", "gx"),
        P("gx", "gy"),
        P("gy", "gx"),
        P("gy", "gx"),
        P("gx", "gy"),
        P("dp", "gx", "gy"),
    )
    return jax.shard_map(
        body,
        mesh=mesh,
        in_specs=placed,
        out_specs=(
            P("dp", "gx", "gy"),
            P("dp", "gx", "gy"),
            P("dp", "gx", "gy"),
            P(),
            P(),
            P("gy", "gx"),
            P("gy", "gx"),
            P("gy", "gx"),
            P("gx", "gy"),
            P("gy", "gx"),
            P("gy", "gx"),
            P("gy", "gx"),
            P("gx", "gy"),
            P("gy", "gx"),
            P("gy", "gx"),
            P("gx", "gy"),
        ),
        check_vma=False,
    )
```

```python
import functools

import jax
import jax.numpy as jnp
from jax import lax
from jax.experimental import pallas as pl
from jax.experimental.pallas import tpu as pltpu
from jax.sharding import PartitionSpec as P

DH = 64
epsilon = 1e-06
masked_score = -1000000000.0
f32 = jnp.float32
bf16 = jnp.bfloat16
VMEM_LIMIT = 48 * 1024 * 1024


def mm(a, b):
    return jnp.dot(a, b, preferred_element_type=f32)


def mm_t(a, b):
    return lax.dot_general(a, b, (((1,), (1,)), ((), ())), preferred_element_type=f32)


def t_mm(a, b):
    return lax.dot_general(a, b, (((0,), (0,)), ((), ())), preferred_element_type=f32)


def shift_gx(value, step):
    n = lax.axis_size("gx")
    return lax.ppermute(value, "gx", [(i, (i + step) % n) for i in range(n)])


def gather_late(own):
    n = lax.axis_size("gx")
    return jnp.concatenate([own] + [shift_gx(own, n - k) for k in range(1, n)], axis=0)


def in_order(cyclic, rows):
    n = lax.axis_size("gx")
    start = lax.rem(n - lax.axis_index("gx"), n) * rows
    return lax.dynamic_slice_in_dim(
        jnp.concatenate([cyclic, cyclic], axis=0), start, n * rows, 0
    )


def scatter_late(slabs):
    total = slabs[0]
    for k in range(1, len(slabs)):
        total = total + shift_gx(slabs[k].astype(bf16), k).astype(f32)
    return total


def mean_last(x):
    return jnp.mean(x, axis=-1, keepdims=True)


def boundary_kernel(mode, n, transposed, *refs):
    mul = mm_t if transposed else mm
    if mode == "first":
        x_ref, gain_ref, rows_ref, ss, rs = refs
    elif mode == "forward":
        left_ref, w_ref, x_ref, gain_ref, out_ref, rows_ref, sent, got, ss, rs = refs
    elif mode == "backward":
        left_ref, w_ref, x_ref, gain_ref, g_ref, out_ref, gg_ref, rows_ref, sent, got, ss, rs = refs
    else:
        left_ref, w_ref, x_ref, gain_ref, g_ref, out_ref, gg_ref, sent, got, ss, rs = refs
    me = lax.axis_index("gx")
    rows = x_ref.shape[0]
    order = sorted(range(1, n), key=lambda d: abs(2 * d - n))
    barrier = pltpu.get_barrier_semaphore()
    for d in range(1, n):
        pl.semaphore_signal(
            barrier,
            inc=1,
            device_id={"gx": lax.rem(me + d, n)},
            device_id_type=pl.DeviceIdType.MESH,
        )
    pl.semaphore_wait(barrier, n - 1)

    def send(source, target, stage, d):
        copy = pltpu.make_async_remote_copy(
            src_ref=source,
            dst_ref=target,
            send_sem=ss.at[stage, d],
            recv_sem=rs.at[stage, d],
            device_id={"gx": lax.rem(me + d, n)},
            device_id_type=pl.DeviceIdType.MESH,
        )
        copy.start()
        return copy

    def part(column):
        at = pl.multiple_of(column * rows, rows)
        return mul(left_ref[pl.ds(at, rows), :], w_ref[...])

    copies = []
    if mode != "first":
        for d in order:
            sent[d] = part(lax.rem(me + d, n)).astype(bf16)
            copies.append(send(sent.at[d], got.at[d], 0, d))
        total = part(me)
        for d, copy in zip(order, copies):
            copy.wait_recv()
            total = total + got[d].astype(f32)
    gain = gain_ref[...]
    if mode in ("first", "forward"):
        stream = x_ref[...] if mode == "first" else x_ref[...] + total
        low = (stream * lax.rsqrt(mean_last(stream * stream) + epsilon) * gain).astype(bf16)
        if mode == "forward":
            out_ref[...] = stream
    else:
        stream = x_ref[...]
        root = lax.rsqrt(mean_last(stream * stream) + epsilon)
        plain = stream * root
        scaled = total * gain
        grad = g_ref[...] + root * (scaled - plain * mean_last(scaled * plain))
        gg_ref[...] = jnp.sum(total * plain, axis=0, keepdims=True)
        out_ref[...] = grad
        low = grad.astype(bf16)
    if mode != "last":
        mine = rows_ref.at[pl.ds(pl.multiple_of(me * rows, rows), rows), :]
        mine[...] = low
        out_copies = [send(mine, mine, 1, d) for d in order]
        for copy in out_copies:
            copy.wait()
    for copy in copies:
        copy.wait_send()


def boundary(mode, cid, operands, transposed=False):
    n = lax.axis_size("gx")
    x = operands[0 if mode == "first" else 2]
    rows, width = x.shape
    shapes = []
    if mode != "first":
        shapes.append(jax.ShapeDtypeStruct((rows, width), f32))
    if mode in ("backward", "last"):
        shapes.append(jax.ShapeDtypeStruct((1, width), f32))
    if mode != "last":
        shapes.append(jax.ShapeDtypeStruct((n * rows, width), bf16))
    scratch = []
    if mode != "first":
        scratch += [pltpu.VMEM((n, rows, width), bf16)] * 2
    scratch += [pltpu.SemaphoreType.DMA((2, n))] * 2
    vm = pl.BlockSpec(memory_space=pltpu.VMEM)
    return pl.pallas_call(
        functools.partial(boundary_kernel, mode, n, transposed),
        out_shape=shapes,
        in_specs=[vm] * len(operands),
        out_specs=[vm] * len(shapes),
        scratch_shapes=scratch,
        compiler_params=pltpu.CompilerParams(
            vmem_limit_bytes=VMEM_LIMIT, collective_id=cid, has_side_effects=True
        ),
        name="boundary_" + mode,
    )(*operands)


def swap_bit(value, axis, bit):
    n = lax.axis_size(axis)
    return lax.ppermute(value, axis, [(i, i ^ (1 << bit)) for i in range(n)])


def sum_small(value):
    for axis in ("gy", "gx", "dp"):
        n = lax.axis_size(axis)
        if n & (n - 1):
            value = lax.psum(value, axis)
        else:
            for bit in range(n.bit_length() - 1):
                value = value + swap_bit(value, axis, bit)
    return value


def over_sequences(value, reverse):
    n = lax.axis_size("dp")
    if n & (n - 1) or value.shape[0] % n:
        return lax.psum(value.astype(bf16), "dp").astype(f32)
    me = lax.axis_index("dp")
    bits = list(range(n.bit_length() - 1))
    if reverse:
        bits = bits[::-1]
    for bit in bits:
        size = value.shape[0] // 2
        upper = (me >> bit) & 1
        other = lax.dynamic_slice_in_dim(value, (1 - upper) * size, size, 0).astype(bf16)
        own = lax.dynamic_slice_in_dim(value, upper * size, size, 0)
        value = own + swap_bit(other, "dp", bit).astype(f32)
    value = value.astype(bf16)
    for bit in bits[::-1]:
        other = swap_bit(value, "dp", bit)
        upper = ((me >> bit) & 1) == 1
        value = jnp.concatenate(
            [jnp.where(upper, other, value), jnp.where(upper, value, other)], axis=0
        )
    return value.astype(f32)


def swap(value):
    size = lax.axis_size("gy")
    return lax.ppermute(value, "gy", [(i, size - 1 - i) for i in range(size)])


def natural_rows(pair_ref, width, start, block):
    pieces = []
    for b in range(2 * (width // (2 * block))):
        pieces.append(pair_ref[b % 2, (b // 2) * block : (b // 2 + 1) * block, start : start + DH])
    return jnp.concatenate(pieces, axis=0)


def softmax_rows(scores):
    top = jnp.max(scores, axis=-1, keepdims=True)
    e = jnp.exp(scores - top)
    return e * (1.0 / jnp.sum(e, axis=-1, keepdims=True))


def bias_tile(vec_ref, head, block):
    row = vec_ref[head : head + 1, :]
    return pltpu.roll(
        jnp.broadcast_to(row, (block, row.shape[1])), 0, 1, stride=1, stride_axis=0
    )


def rotate_lanes(x, amount):
    if amount == 0:
        return x
    width = x.shape[1]
    return jnp.concatenate([x[:, width - amount :], x[:, : width - amount]], axis=1)


def self_mask(core_ref, dq_ref, dk_ref, g, width, block):
    first = (2 * g + core_ref[0]) * block
    rows = first + lax.broadcasted_iota(jnp.int32, (block, width), 0)
    cols = lax.broadcasted_iota(jnp.int32, (block, width), 1)
    own = dq_ref[g * block : (g + 1) * block, :]
    return (cols <= rows) & (own == dk_ref[:, :width])


def self_scores(q, k, tile, mask, g, width, block):
    return jnp.where(mask, mm_t(q, k) + rotate_lanes(tile, 2 * block * g)[:, :width], masked_score)


def self_forward_kernel(block, heads, core_ref, q_ref, kv_ref, dq_ref, dk_ref, vec_ref, out_ref):
    groups = q_ref.shape[0] // block
    keys = 2 * q_ref.shape[0]
    masks = [
        self_mask(core_ref, dq_ref, dk_ref, g, 2 * block * (g + 1), block) for g in range(groups)
    ]
    parts = [[] for _ in range(groups)]
    for h in range(heads):
        k = natural_rows(kv_ref, keys, h * DH, block)
        v = natural_rows(kv_ref, keys, (heads + h) * DH, block)
        tile = bias_tile(vec_ref, h, block)
        for g in range(groups):
            width = 2 * block * (g + 1)
            q = q_ref[g * block : (g + 1) * block, h * DH : (h + 1) * DH]
            p = softmax_rows(self_scores(q, k[:width], tile, masks[g], g, width, block))
            parts[g].append(mm(p.astype(bf16), v[:width]))
    for g in range(groups):
        out_ref[g * block : (g + 1) * block, :] = jnp.concatenate(parts[g], axis=1).astype(bf16)


def self_backward_kernel(
    block, heads, core_ref, q_ref, kv_ref, dq_ref, dk_ref, vec_ref, dc_ref, gq_ref, gkv_ref, gd_ref
):
    groups = q_ref.shape[0] // block
    keys = 2 * q_ref.shape[0]
    masks = [
        self_mask(core_ref, dq_ref, dk_ref, g, 2 * block * (g + 1), block) for g in range(groups)
    ]
    flip = (
        lax.broadcasted_iota(jnp.int32, (block, block), 0)
        + lax.broadcasted_iota(jnp.int32, (block, block), 1)
        == block - 1
    ).astype(bf16)
    parts = [[] for _ in range(groups)]
    gd_ref[...] = jnp.zeros_like(gd_ref)
    for h in range(heads):
        k = natural_rows(kv_ref, keys, h * DH, block)
        v = natural_rows(kv_ref, keys, (heads + h) * DH, block)
        tile = bias_tile(vec_ref, h, block)
        gk_total = None
        gv_total = None
        shifted = None
        for g in range(groups - 1, -1, -1):
            width = 2 * block * (g + 1)
            q = q_ref[g * block : (g + 1) * block, h * DH : (h + 1) * DH]
            dc = dc_ref[g * block : (g + 1) * block, h * DH : (h + 1) * DH]
            p = softmax_rows(self_scores(q, k[:width], tile, masks[g], g, width, block))
            dp = mm_t(dc, v[:width])
            inner = jnp.sum(dp * p, axis=-1, keepdims=True)
            ds = (p * (dp - inner)).astype(bf16)
            parts[g].append(mm(ds, k[:width]))
            gk = t_mm(q, ds)
            gv = t_mm(dc, p.astype(bf16))
            flipped = mm(flip, ds)
            if gk_total is None:
                gk_total, gv_total = gk, gv
                shifted = rotate_lanes(flipped, keys - 2 * block * g) if g else flipped
            else:
                rest = jnp.zeros((DH, keys - width), f32)
                gk_total = gk_total + jnp.concatenate([gk, rest], axis=1)
                gv_total = gv_total + jnp.concatenate([gv, rest], axis=1)
                flipped = jnp.concatenate(
                    [flipped, jnp.zeros((block, keys - width), f32)], axis=1
                )
                if g:
                    flipped = rotate_lanes(flipped, keys - 2 * block * g)
                shifted = shifted + flipped
        for b in range(2 * groups):
            lanes = slice((b // 2) * block, (b // 2 + 1) * block)
            source = slice(b * block, (b + 1) * block)
            gkv_ref[b % 2, h * DH : (h + 1) * DH, lanes] = gk_total[:, source].astype(bf16)
            gkv_ref[b % 2, (heads + h) * DH : (heads + h + 1) * DH, lanes] = gv_total[
                :, source
            ].astype(bf16)
        gd_ref[h : h + 1, :] = jnp.sum(
            pltpu.roll(shifted, 0, 1, stride=1, stride_axis=0), axis=0, keepdims=True
        )
    for g in range(groups):
        gq_ref[g * block : (g + 1) * block, :] = jnp.concatenate(parts[g], axis=1).astype(bf16)


def cross_forward_kernel(block, heads, q_ref, kv_ref, out_ref):
    rows = q_ref.shape[0]
    for h in range(heads):
        k = jnp.concatenate([kv_ref[c, :, h * DH : (h + 1) * DH] for c in range(2)], axis=0)
        v = jnp.concatenate(
            [kv_ref[c, :, (heads + h) * DH : (heads + h + 1) * DH] for c in range(2)], axis=0
        )
        for r in range(0, rows, block):
            p = softmax_rows(mm_t(q_ref[r : r + block, h * DH : (h + 1) * DH], k))
            out_ref[r : r + block, h * DH : (h + 1) * DH] = mm(p.astype(bf16), v).astype(bf16)


def cross_backward_kernel(block, heads, q_ref, kv_ref, dc_ref, gq_ref, gkv_ref):
    rows = q_ref.shape[0]
    for h in range(heads):
        k = jnp.concatenate([kv_ref[c, :, h * DH : (h + 1) * DH] for c in range(2)], axis=0)
        v = jnp.concatenate(
            [kv_ref[c, :, (heads + h) * DH : (heads + h + 1) * DH] for c in range(2)], axis=0
        )
        gk_total = None
        for r in range(0, rows, block):
            q = q_ref[r : r + block, h * DH : (h + 1) * DH]
            dc = dc_ref[r : r + block, h * DH : (h + 1) * DH]
            p = softmax_rows(mm_t(q, k))
            dp = mm_t(dc, v)
            inner = jnp.sum(dp * p, axis=-1, keepdims=True)
            ds = (p * (dp - inner)).astype(bf16)
            gq_ref[r : r + block, h * DH : (h + 1) * DH] = mm(ds, k).astype(bf16)
            gk = t_mm(q, ds)
            gv = t_mm(dc, p.astype(bf16))
            gk_total = gk if gk_total is None else gk_total + gk
            gv_total = gv if r == 0 else gv_total + gv
        for c in range(2):
            source = slice(c * rows, (c + 1) * rows)
            gkv_ref[c, h * DH : (h + 1) * DH, :] = gk_total[:, source].astype(bf16)
            gkv_ref[c, (heads + h) * DH : (heads + h + 1) * DH, :] = gv_total[:, source].astype(
                bf16
            )


def call(kernel, out_shape, smem, name):
    vm = pl.BlockSpec(memory_space=pltpu.VMEM)

    def run(*operands):
        specs = [pl.BlockSpec(memory_space=pltpu.SMEM)] * smem + [vm] * (len(operands) - smem)
        multi = isinstance(out_shape, (list, tuple))
        return pl.pallas_call(
            kernel,
            out_shape=out_shape,
            in_specs=specs,
            out_specs=[vm] * len(out_shape) if multi else vm,
            compiler_params=pltpu.CompilerParams(vmem_limit_bytes=VMEM_LIMIT),
            name=name,
        )(*operands)

    return run


def glu_piece(gate, up_part):
    return jax.nn.gelu(gate, approximate=True) * up_part


def body(
    hidden_in,
    encoded,
    doc_ids,
    buckets,
    rel_table,
    norm_gains,
    self_q,
    self_k,
    self_v,
    self_out,
    cross_q,
    cross_k,
    cross_v,
    cross_out,
    ff_gate,
    ff_up,
    ff_down,
    grad_out,
):
    core = lax.axis_index("gy")
    column = lax.axis_index("gx")
    groups = lax.axis_size("gx")
    seq_len = doc_ids.shape[1]
    half = hidden_in.shape[2]
    block = hidden_in.shape[1] // 2
    proj = self_q.shape[1]
    heads = proj // DH
    hid_part = ff_gate.shape[1]
    own_tokens = groups * block
    core_one = core.reshape(1).astype(jnp.int32)

    def to_rows(x):
        return lax.all_to_all(x, "gy", x.ndim - 2, x.ndim - 1, tiled=True)

    def to_features(x):
        return lax.all_to_all(x, "gy", x.ndim - 1, x.ndim - 2, tiled=True)

    first_rows = to_rows(hidden_in[0])
    w_self = lax.all_gather(
        jnp.concatenate([self_q, self_k, self_v], axis=1), "gy", axis=0, tiled=True
    )
    both_rows = to_rows(jnp.concatenate([encoded, grad_out], axis=0))
    w_cross = lax.all_gather(
        jnp.concatenate([cross_q, cross_k, cross_v], axis=1), "gy", axis=0, tiled=True
    )
    w_ff = lax.all_gather(jnp.concatenate([ff_gate, ff_up], axis=1), "gy", axis=0, tiled=True)
    w_outs = lax.all_gather(
        jnp.concatenate([self_out, cross_out, ff_down], axis=0), "gy", axis=1, tiled=True
    )
    w_self_out, w_cross_out, w_down = (
        w_outs[:proj],
        w_outs[proj : 2 * proj],
        w_outs[2 * proj :],
    )
    w_cq, w_ckv = w_cross[:, :proj], w_cross[:, proj:]

    twice = jnp.concatenate([buckets, buckets])

    def reversed_window(start):
        return lax.dynamic_slice_in_dim(twice, start, seq_len, 0)[::-1]

    table_part = lax.dynamic_slice_in_dim(rel_table, column * heads, heads, 1)

    def hot(near):
        return (
            near[None, :]
            == jnp.arange(rel_table.shape[0], dtype=jnp.int32)[:, None]
        ).astype(f32)

    bias_vec = lax.dot_general(
        table_part,
        hot(reversed_window(core * block + 1)),
        (((0,), (0,)), ((), ())),
        precision=lax.Precision.HIGHEST,
    )
    docs_k = doc_ids
    docs_q = lax.dynamic_index_in_dim(
        doc_ids.reshape(groups, 2, block), core, 1, keepdims=False
    ).reshape(own_tokens, 1)

    stream0 = first_rows.astype(f32)
    gains_in = [norm_gains[i : i + 1] for i in range(3)]
    (rows_one,) = boundary("first", 1, (stream0, gains_in[0]))
    qkv = mm(rows_one, w_self).astype(bf16)
    q1 = qkv[:, :proj]
    kv1 = lax.all_gather(qkv[:, proj:], "gy", axis=0)

    enc_rows = gather_late(both_rows[0])
    kv2_own = mm(enc_rows, w_ckv).astype(bf16)
    kv2 = lax.all_gather(kv2_own, "gy", axis=0)
    out_rows = in_order(gather_late(both_rows[1]), block)
    d_hid = mm_t(out_rows, w_down)

    ctx1 = call(
        functools.partial(self_forward_kernel, block, heads),
        jax.ShapeDtypeStruct((own_tokens, proj), bf16),
        1,
        "self_forward",
    )(core_one, q1, kv1, docs_q, docs_k, bias_vec)
    stream1, rows_two = boundary("forward", 2, (ctx1, w_self_out, stream0, gains_in[1]))
    q2 = mm(rows_two, w_cq).astype(bf16)
    ctx2 = call(
        functools.partial(cross_forward_kernel, 2 * block, heads),
        jax.ShapeDtypeStruct((own_tokens, proj), bf16),
        0,
        "cross_forward",
    )(q2, kv2)
    stream2, rows_three = boundary("forward", 3, (ctx2, w_cross_out, stream1, gains_in[2]))
    gate_up = mm(rows_three, w_ff)
    hidden_float, glu_pull = jax.vjp(glu_piece, gate_up[:, :hid_part], gate_up[:, hid_part:])
    hid = hidden_float.astype(bf16)
    d_gate, d_up = glu_pull(d_hid)
    d_gu = jnp.concatenate([d_gate, d_up], axis=1).astype(bf16)

    def own_half(x, which):
        return lax.dynamic_slice_in_dim(x, which * half, half, 1)

    def grad_cols(rows, d):
        other = t_mm(own_half(rows, 1 - core), d).astype(bf16)
        return t_mm(own_half(rows, core), d) + swap(other).astype(f32)

    def grad_rows(left, rows):
        other = t_mm(left, own_half(rows, 1 - core)).astype(bf16)
        return t_mm(left, own_half(rows, core)) + swap(other).astype(f32)

    g2, gain_three, rows_a2 = boundary(
        "backward", 4, (d_gu, w_ff, stream2, gains_in[2], both_rows[1].astype(f32)), True
    )

    def slab_at(x, k):
        at = lax.rem(column + k, groups) * block
        return lax.dynamic_slice_in_dim(x, at, block, 0)

    layer_sum = scatter_late([mm(slab_at(hid, k), w_down) for k in range(groups)])
    layer_out = to_features((stream2 + layer_sum).astype(bf16))[None]
    g_gu = grad_cols(rows_three, d_gu)
    g_down = grad_rows(hid, out_rows)
    dctx2 = mm_t(rows_a2, w_cross_out).astype(bf16)
    dq2, dkv2_both = call(
        functools.partial(cross_backward_kernel, 2 * block, heads),
        (
            jax.ShapeDtypeStruct((own_tokens, proj), bf16),
            jax.ShapeDtypeStruct((2, 2 * proj, own_tokens), bf16),
        ),
        0,
        "cross_backward",
    )(q2, kv2, dctx2)

    def pair_sum(both):
        other = lax.dynamic_index_in_dim(both, 1 - core, 0, keepdims=False)
        own = lax.dynamic_index_in_dim(both, core, 0, keepdims=False)
        return (own.astype(f32) + swap(other).astype(f32)).astype(bf16)

    dkv2 = pair_sum(dkv2_both)
    g1, gain_two, rows_a1 = boundary(
        "backward", 5, (dq2, w_cq, stream1, gains_in[1], g2), True
    )
    dctx1 = mm_t(rows_a1, w_self_out).astype(bf16)
    enc_slabs = [
        lax.dot_general(
            dkv2[:, k * block : (k + 1) * block],
            w_ckv,
            (((0,), (1,)), ((), ())),
            preferred_element_type=f32,
        )
        for k in range(groups)
    ]
    grad_encoded = to_features(scatter_late(enc_slabs))[None]
    g_cq = grad_cols(rows_two, dq2)

    def grad_cols_t(rows, d_t):
        other = mm(d_t, own_half(rows, 1 - core)).astype(bf16)
        return (mm(d_t, own_half(rows, core)) + swap(other).astype(f32)).T

    g_ckv = grad_cols_t(enc_rows, dkv2)
    g_cross_out = grad_rows(ctx2, rows_a2)

    dq1, dkv1_both, by_shift = call(
        functools.partial(self_backward_kernel, block, heads),
        (
            jax.ShapeDtypeStruct((own_tokens, proj), bf16),
            jax.ShapeDtypeStruct((2, 2 * proj, own_tokens), bf16),
            jax.ShapeDtypeStruct((8, seq_len), f32),
        ),
        1,
        "self_backward",
    )(core_one, q1, kv1, docs_q, docs_k, bias_vec, dctx1)
    dkv1 = pair_sum(dkv1_both)
    dqkv1 = jnp.concatenate([dq1, dkv1.T], axis=1)
    g0, gain_one = boundary("last", 6, (dqkv1, w_self, stream0, gains_in[0], g1), True)
    grad_hidden = to_features(g0)[None]
    g_qkv = grad_cols(rows_one, dqkv1)
    g_self_out = grad_rows(ctx1, rows_a1)

    table_grad = lax.dot_general(
        hot(reversed_window(core * block + block)),
        by_shift[:heads],
        (((1,), (1,)), ((), ())),
        precision=lax.Precision.HIGHEST,
    )
    rel_full = lax.dynamic_update_slice(
        jnp.zeros(rel_table.shape, f32), table_grad, (0, column * heads)
    )
    flat = jnp.concatenate(
        [x.reshape(-1) for x in (gain_one, gain_two, gain_three, rel_full)]
    )
    flat = sum_small(flat.reshape(-1, 128)).reshape(-1)
    grad_gains = flat[: norm_gains.size].reshape(norm_gains.shape)
    grad_rel = flat[norm_gains.size :].reshape(rel_table.shape)

    s_gate = over_sequences(g_gu[:, :hid_part], False)
    s_up = over_sequences(g_gu[:, hid_part:], True)
    s_down = over_sequences(g_down, False)
    s_cq = over_sequences(jnp.concatenate([g_cq, g_cross_out.reshape(half, proj)], axis=1), True)
    s_ckv = over_sequences(g_ckv, False)
    s_q = over_sequences(
        jnp.concatenate([g_qkv[:, :proj], g_self_out.reshape(half, proj)], axis=1), True
    )
    s_kv = over_sequences(g_qkv[:, proj:], False)
    return (
        layer_out,
        grad_hidden,
        grad_encoded,
        grad_gains,
        grad_rel,
        s_q[:, :proj],
        s_kv[:, :proj],
        s_kv[:, proj:],
        s_q[:, proj:].reshape(proj, half),
        s_cq[:, :proj],
        s_ckv[:, :proj],
        s_ckv[:, proj:],
        s_cq[:, proj:].reshape(proj, half),
        s_gate,
        s_up,
        s_down,
    )


def solution(mesh):
    placed = (
        P("dp", "gx", "gy"),
        P("dp", "gx", "gy"),
        P("dp", None),
        P(),
        P(),
        P(),
        P("gy", "gx"),
        P("gy", "gx"),
        P("gy", "gx"),
        P("gx", "gy"),
        P("gy", "gx"),
        P("gy", "gx"),
        P("gy", "gx"),
        P("gx", "gy"),
        P("gy", "gx"),
        P("gy", "gx"),
        P("gx", "gy"),
        P("dp", "gx", "gy"),
    )
    return jax.shard_map(
        body,
        mesh=mesh,
        in_specs=placed,
        out_specs=(
            P("dp", "gx", "gy"),
            P("dp", "gx", "gy"),
            P("dp", "gx", "gy"),
            P(),
            P(),
            P("gy", "gx"),
            P("gy", "gx"),
            P("gy", "gx"),
            P("gx", "gy"),
            P("gy", "gx"),
            P("gy", "gx"),
            P("gy", "gx"),
            P("gx", "gy"),
            P("gy", "gx"),
            P("gy", "gx"),
            P("gx", "gy"),
        ),
        check_vma=False,
    )
```

```python
import functools

import jax
import jax.numpy as jnp
from jax import lax
from jax.experimental import pallas as pl
from jax.experimental.pallas import tpu as pltpu
from jax.sharding import PartitionSpec as P

DH = 64
epsilon = 1e-06
masked_score = -1000000000.0
f32 = jnp.float32
bf16 = jnp.bfloat16
VMEM_LIMIT = 48 * 1024 * 1024


def mm(a, b):
    return jnp.dot(a, b, preferred_element_type=f32)


def mm_t(a, b):
    return lax.dot_general(a, b, (((1,), (1,)), ((), ())), preferred_element_type=f32)


def t_mm(a, b):
    return lax.dot_general(a, b, (((0,), (0,)), ((), ())), preferred_element_type=f32)


def shift_gx(value, step):
    n = lax.axis_size("gx")
    return lax.ppermute(value, "gx", [(i, (i + step) % n) for i in range(n)])


def gather_late(own):
    n = lax.axis_size("gx")
    return jnp.concatenate([own] + [shift_gx(own, n - k) for k in range(1, n)], axis=0)


def in_order(cyclic, rows):
    n = lax.axis_size("gx")
    start = lax.rem(n - lax.axis_index("gx"), n) * rows
    return lax.dynamic_slice_in_dim(
        jnp.concatenate([cyclic, cyclic], axis=0), start, n * rows, 0
    )


def scatter_late(slabs):
    total = slabs[0]
    for k in range(1, len(slabs)):
        total = total + shift_gx(slabs[k].astype(bf16), k).astype(f32)
    return total


def swap(value):
    size = lax.axis_size("gy")
    return lax.ppermute(value, "gy", [(i, size - 1 - i) for i in range(size)])


def mean_last(x):
    return jnp.mean(x, axis=-1, keepdims=True)


def peer(axis, me, d, n):
    return {axis: lax.rem(me + d, n)}


def greet(axes):
    barrier = pltpu.get_barrier_semaphore()
    count = 0
    for axis, n in axes:
        me = lax.axis_index(axis)
        for d in range(1, n):
            pl.semaphore_signal(
                barrier,
                inc=1,
                device_id=peer(axis, me, d, n),
                device_id_type=pl.DeviceIdType.MESH,
            )
        count += n - 1
    pl.semaphore_wait(barrier, count)


def start_copy(source, target, send_sem, recv_sem, device):
    copy = pltpu.make_async_remote_copy(
        src_ref=source,
        dst_ref=target,
        send_sem=send_sem,
        recv_sem=recv_sem,
        device_id=device,
        device_id_type=pl.DeviceIdType.MESH,
    )
    copy.start()
    return copy


class SequenceSum:
    def __init__(self, n, value_ref, total_ref, got, ss, rs):
        self.n, self.value, self.total, self.got = n, value_ref, total_ref, got
        self.ss, self.rs = ss, rs
        self.me = lax.axis_index("dp")
        self.rows = value_ref.shape[0] // n

    def slab(self, ref, index):
        return ref.at[pl.ds(pl.multiple_of(index * self.rows, self.rows), self.rows), :]

    def send(self):
        self.copies = [
            start_copy(
                self.slab(self.value, lax.rem(self.me + d, self.n)),
                self.got.at[d],
                self.ss.at[0, d],
                self.rs.at[0, d],
                peer("dp", self.me, d, self.n),
            )
            for d in range(1, self.n)
        ]

    def add(self):
        total = self.slab(self.value, self.me)[...].astype(f32)
        for d, copy in zip(range(1, self.n), self.copies):
            copy.wait_recv()
            total = total + self.got[d].astype(f32)
        mine = self.slab(self.total, self.me)
        mine[...] = total.astype(bf16)
        self.back = [
            start_copy(
                mine, mine, self.ss.at[1, d], self.rs.at[1, d], peer("dp", self.me, d, self.n)
            )
            for d in range(1, self.n)
        ]

    def finish(self):
        for copy in self.back:
            copy.wait()
        for copy in self.copies:
            copy.wait_send()


def boundary_kernel(mode, n, seqs, transposed, *refs):
    mul = mm_t if transposed else mm
    rider = None
    if seqs:
        *refs, dp_got, dp_ss, dp_rs = refs
    if mode == "first":
        x_ref, gain_ref, rows_ref, ss, rs = refs
    elif mode == "forward":
        left_ref, w_ref, x_ref, gain_ref, out_ref, rows_ref, sent, got, ss, rs = refs
    elif mode == "backward" and not seqs:
        left_ref, w_ref, x_ref, gain_ref, g_ref, out_ref, gg_ref, rows_ref, sent, got, ss, rs = refs
    elif mode == "backward":
        (left_ref, w_ref, x_ref, gain_ref, g_ref, value_ref) = refs[:6]
        (out_ref, gg_ref, rows_ref, total_ref, sent, got, ss, rs) = refs[6:]
    else:
        (left_ref, w_ref, x_ref, gain_ref, g_ref, value_ref) = refs[:6]
        (out_ref, gg_ref, total_ref, sent, got, ss, rs) = refs[6:]
    me = lax.axis_index("gx")
    rows = x_ref.shape[0]
    order = sorted(range(1, n), key=lambda d: abs(2 * d - n))
    greet([("gx", n)] + ([("dp", seqs)] if seqs else []))
    if seqs:
        rider = SequenceSum(seqs, value_ref, total_ref, dp_got, dp_ss, dp_rs)
        rider.send()

    def part(column):
        at = pl.multiple_of(column * rows, rows)
        return mul(left_ref[pl.ds(at, rows), :], w_ref[...])

    copies = []
    if mode != "first":
        for d in order:
            sent[d] = part(lax.rem(me + d, n)).astype(bf16)
            copies.append(
                start_copy(sent.at[d], got.at[d], ss.at[0, d], rs.at[0, d], peer("gx", me, d, n))
            )
        total = part(me)
        for d, copy in zip(order, copies):
            copy.wait_recv()
            total = total + got[d].astype(f32)
    gain = gain_ref[...]
    if mode in ("first", "forward"):
        stream = x_ref[...] if mode == "first" else x_ref[...] + total
        low = (stream * lax.rsqrt(mean_last(stream * stream) + epsilon) * gain).astype(bf16)
        if mode == "forward":
            out_ref[...] = stream
    else:
        stream = x_ref[...]
        root = lax.rsqrt(mean_last(stream * stream) + epsilon)
        plain = stream * root
        scaled = total * gain
        grad = g_ref[...] + root * (scaled - plain * mean_last(scaled * plain))
        gg_ref[...] = jnp.sum(total * plain, axis=0, keepdims=True)
        out_ref[...] = grad
        low = grad.astype(bf16)
    out_copies = []
    if mode != "last":
        mine = rows_ref.at[pl.ds(pl.multiple_of(me * rows, rows), rows), :]
        mine[...] = low
        out_copies = [
            start_copy(mine, mine, ss.at[1, d], rs.at[1, d], peer("gx", me, d, n)) for d in order
        ]
    if rider:
        rider.add()
    for copy in out_copies:
        copy.wait()
    for copy in copies:
        copy.wait_send()
    if rider:
        rider.finish()


def boundary(mode, cid, operands, transposed=False, value=None):
    n = lax.axis_size("gx")
    seqs = lax.axis_size("dp") if value is not None else 0
    x = operands[0 if mode == "first" else 2]
    rows, width = x.shape
    shapes = []
    if mode != "first":
        shapes.append(jax.ShapeDtypeStruct((rows, width), f32))
    if mode in ("backward", "last"):
        shapes.append(jax.ShapeDtypeStruct((1, width), f32))
    if mode != "last":
        shapes.append(jax.ShapeDtypeStruct((n * rows, width), bf16))
    scratch = []
    if mode != "first":
        scratch += [pltpu.VMEM((n, rows, width), bf16)] * 2
    scratch += [pltpu.SemaphoreType.DMA((2, n))] * 2
    if seqs:
        operands = operands + (value,)
        shapes.append(jax.ShapeDtypeStruct(value.shape, bf16))
        scratch.append(pltpu.VMEM((seqs, value.shape[0] // seqs, value.shape[1]), bf16))
        scratch += [pltpu.SemaphoreType.DMA((2, seqs))] * 2
    vm = pl.BlockSpec(memory_space=pltpu.VMEM)
    return pl.pallas_call(
        functools.partial(boundary_kernel, mode, n, seqs, transposed),
        out_shape=shapes,
        in_specs=[vm] * len(operands),
        out_specs=[vm] * len(shapes),
        scratch_shapes=scratch,
        compiler_params=pltpu.CompilerParams(
            vmem_limit_bytes=VMEM_LIMIT, collective_id=cid, has_side_effects=True
        ),
        name="boundary_" + mode,
    )(*operands)


def final_kernel(seqs, axes, value_ref, small_ref, total_ref, sum_ref, *scratch):
    dp_got, dp_ss, dp_rs = scratch[:3]
    greet(axes)
    rider = SequenceSum(seqs, value_ref, total_ref, dp_got, dp_ss, dp_rs)
    rider.send()
    for step, (axis, n) in enumerate(axes):
        got, ss, rs = scratch[3 + 3 * step : 6 + 3 * step]
        me = lax.axis_index(axis)
        mine = got.at[me]
        mine[...] = small_ref[...] if step == 0 else partial_sum
        copies = [
            start_copy(mine, mine, ss.at[d], rs.at[d], peer(axis, me, d, n)) for d in range(1, n)
        ]
        for copy in copies:
            copy.wait()
        partial_sum = got[0]
        for source in range(1, n):
            partial_sum = partial_sum + got[source]
    sum_ref[...] = partial_sum
    rider.add()
    rider.finish()


def final_sums(cid, value, small):
    axes = [(axis, lax.axis_size(axis)) for axis in ("gy", "gx", "dp")]
    seqs = lax.axis_size("dp")
    scratch = [pltpu.VMEM((seqs, value.shape[0] // seqs, value.shape[1]), bf16)]
    scratch += [pltpu.SemaphoreType.DMA((2, seqs))] * 2
    for _, n in axes:
        scratch.append(pltpu.VMEM((n,) + small.shape, f32))
        scratch += [pltpu.SemaphoreType.DMA((n,))] * 2
    vm = pl.BlockSpec(memory_space=pltpu.VMEM)
    return pl.pallas_call(
        functools.partial(final_kernel, seqs, axes),
        out_shape=[
            jax.ShapeDtypeStruct(value.shape, bf16),
            jax.ShapeDtypeStruct(small.shape, f32),
        ],
        in_specs=[vm, vm],
        out_specs=[vm, vm],
        scratch_shapes=scratch,
        compiler_params=pltpu.CompilerParams(
            vmem_limit_bytes=VMEM_LIMIT, collective_id=cid, has_side_effects=True
        ),
        name="final_sums",
    )(value, small)


def pad_rows(value, multiple):
    return jnp.pad(value, ((0, -value.shape[0] % multiple), (0, 0)))


def natural_rows(pair_ref, width, start, block):
    pieces = []
    for b in range(2 * (width // (2 * block))):
        pieces.append(pair_ref[b % 2, (b // 2) * block : (b // 2 + 1) * block, start : start + DH])
    return jnp.concatenate(pieces, axis=0)


def softmax_rows(scores):
    top = jnp.max(scores, axis=-1, keepdims=True)
    e = jnp.exp(scores - top)
    return e * (1.0 / jnp.sum(e, axis=-1, keepdims=True))


def bias_tile(vec_ref, head, block):
    row = vec_ref[head : head + 1, :]
    return pltpu.roll(
        jnp.broadcast_to(row, (block, row.shape[1])), 0, 1, stride=1, stride_axis=0
    )


def rotate_lanes(x, amount):
    if amount == 0:
        return x
    width = x.shape[1]
    return jnp.concatenate([x[:, width - amount :], x[:, : width - amount]], axis=1)


def self_mask(core_ref, dq_ref, dk_ref, g, width, block):
    first = (2 * g + core_ref[0]) * block
    rows = first + lax.broadcasted_iota(jnp.int32, (block, width), 0)
    cols = lax.broadcasted_iota(jnp.int32, (block, width), 1)
    own = dq_ref[g * block : (g + 1) * block, :]
    return (cols <= rows) & (own == dk_ref[:, :width])


def self_scores(q, k, tile, mask, g, width, block):
    return jnp.where(mask, mm_t(q, k) + rotate_lanes(tile, 2 * block * g)[:, :width], masked_score)


def self_forward_kernel(block, heads, core_ref, q_ref, kv_ref, dq_ref, dk_ref, vec_ref, out_ref):
    groups = q_ref.shape[0] // block
    keys = 2 * q_ref.shape[0]
    masks = [
        self_mask(core_ref, dq_ref, dk_ref, g, 2 * block * (g + 1), block) for g in range(groups)
    ]
    parts = [[] for _ in range(groups)]
    for h in range(heads):
        k = natural_rows(kv_ref, keys, h * DH, block)
        v = natural_rows(kv_ref, keys, (heads + h) * DH, block)
        tile = bias_tile(vec_ref, h, block)
        for g in range(groups):
            width = 2 * block * (g + 1)
            q = q_ref[g * block : (g + 1) * block, h * DH : (h + 1) * DH]
            p = softmax_rows(self_scores(q, k[:width], tile, masks[g], g, width, block))
            parts[g].append(mm(p.astype(bf16), v[:width]))
    for g in range(groups):
        out_ref[g * block : (g + 1) * block, :] = jnp.concatenate(parts[g], axis=1).astype(bf16)


def self_backward_kernel(
    block, heads, core_ref, q_ref, kv_ref, dq_ref, dk_ref, vec_ref, dc_ref, gq_ref, gkv_ref, gd_ref
):
    groups = q_ref.shape[0] // block
    keys = 2 * q_ref.shape[0]
    masks = [
        self_mask(core_ref, dq_ref, dk_ref, g, 2 * block * (g + 1), block) for g in range(groups)
    ]
    flip = (
        lax.broadcasted_iota(jnp.int32, (block, block), 0)
        + lax.broadcasted_iota(jnp.int32, (block, block), 1)
        == block - 1
    ).astype(bf16)
    parts = [[] for _ in range(groups)]
    gd_ref[...] = jnp.zeros_like(gd_ref)
    for h in range(heads):
        k = natural_rows(kv_ref, keys, h * DH, block)
        v = natural_rows(kv_ref, keys, (heads + h) * DH, block)
        tile = bias_tile(vec_ref, h, block)
        gk_total = None
        gv_total = None
        shifted = None
        for g in range(groups - 1, -1, -1):
            width = 2 * block * (g + 1)
            q = q_ref[g * block : (g + 1) * block, h * DH : (h + 1) * DH]
            dc = dc_ref[g * block : (g + 1) * block, h * DH : (h + 1) * DH]
            p = softmax_rows(self_scores(q, k[:width], tile, masks[g], g, width, block))
            dp = mm_t(dc, v[:width])
            inner = jnp.sum(dp * p, axis=-1, keepdims=True)
            ds = (p * (dp - inner)).astype(bf16)
            parts[g].append(mm(ds, k[:width]))
            gk = t_mm(q, ds)
            gv = t_mm(dc, p.astype(bf16))
            flipped = mm(flip, ds)
            if gk_total is None:
                gk_total, gv_total = gk, gv
                shifted = rotate_lanes(flipped, keys - 2 * block * g) if g else flipped
            else:
                rest = jnp.zeros((DH, keys - width), f32)
                gk_total = gk_total + jnp.concatenate([gk, rest], axis=1)
                gv_total = gv_total + jnp.concatenate([gv, rest], axis=1)
                flipped = jnp.concatenate(
                    [flipped, jnp.zeros((block, keys - width), f32)], axis=1
                )
                if g:
                    flipped = rotate_lanes(flipped, keys - 2 * block * g)
                shifted = shifted + flipped
        for b in range(2 * groups):
            lanes = slice((b // 2) * block, (b // 2 + 1) * block)
            source = slice(b * block, (b + 1) * block)
            gkv_ref[b % 2, h * DH : (h + 1) * DH, lanes] = gk_total[:, source].astype(bf16)
            gkv_ref[b % 2, (heads + h) * DH : (heads + h + 1) * DH, lanes] = gv_total[
                :, source
            ].astype(bf16)
        gd_ref[h : h + 1, :] = jnp.sum(
            pltpu.roll(shifted, 0, 1, stride=1, stride_axis=0), axis=0, keepdims=True
        )
    for g in range(groups):
        gq_ref[g * block : (g + 1) * block, :] = jnp.concatenate(parts[g], axis=1).astype(bf16)


def cross_forward_kernel(block, heads, q_ref, kv_ref, out_ref):
    rows = q_ref.shape[0]
    for h in range(heads):
        k = jnp.concatenate([kv_ref[c, :, h * DH : (h + 1) * DH] for c in range(2)], axis=0)
        v = jnp.concatenate(
            [kv_ref[c, :, (heads + h) * DH : (heads + h + 1) * DH] for c in range(2)], axis=0
        )
        for r in range(0, rows, block):
            p = softmax_rows(mm_t(q_ref[r : r + block, h * DH : (h + 1) * DH], k))
            out_ref[r : r + block, h * DH : (h + 1) * DH] = mm(p.astype(bf16), v).astype(bf16)


def cross_backward_kernel(block, heads, q_ref, kv_ref, dc_ref, gq_ref, gkv_ref):
    rows = q_ref.shape[0]
    for h in range(heads):
        k = jnp.concatenate([kv_ref[c, :, h * DH : (h + 1) * DH] for c in range(2)], axis=0)
        v = jnp.concatenate(
            [kv_ref[c, :, (heads + h) * DH : (heads + h + 1) * DH] for c in range(2)], axis=0
        )
        gk_total = None
        for r in range(0, rows, block):
            q = q_ref[r : r + block, h * DH : (h + 1) * DH]
            dc = dc_ref[r : r + block, h * DH : (h + 1) * DH]
            p = softmax_rows(mm_t(q, k))
            dp = mm_t(dc, v)
            inner = jnp.sum(dp * p, axis=-1, keepdims=True)
            ds = (p * (dp - inner)).astype(bf16)
            gq_ref[r : r + block, h * DH : (h + 1) * DH] = mm(ds, k).astype(bf16)
            gk = t_mm(q, ds)
            gv = t_mm(dc, p.astype(bf16))
            gk_total = gk if gk_total is None else gk_total + gk
            gv_total = gv if r == 0 else gv_total + gv
        for c in range(2):
            source = slice(c * rows, (c + 1) * rows)
            gkv_ref[c, h * DH : (h + 1) * DH, :] = gk_total[:, source].astype(bf16)
            gkv_ref[c, (heads + h) * DH : (heads + h + 1) * DH, :] = gv_total[:, source].astype(
                bf16
            )


def call(kernel, out_shape, smem, name):
    vm = pl.BlockSpec(memory_space=pltpu.VMEM)

    def run(*operands):
        specs = [pl.BlockSpec(memory_space=pltpu.SMEM)] * smem + [vm] * (len(operands) - smem)
        multi = isinstance(out_shape, (list, tuple))
        return pl.pallas_call(
            kernel,
            out_shape=out_shape,
            in_specs=specs,
            out_specs=[vm] * len(out_shape) if multi else vm,
            compiler_params=pltpu.CompilerParams(vmem_limit_bytes=VMEM_LIMIT),
            name=name,
        )(*operands)

    return run


def glu_piece(gate, up_part):
    return jax.nn.gelu(gate, approximate=True) * up_part


def body(
    hidden_in,
    encoded,
    doc_ids,
    buckets,
    rel_table,
    norm_gains,
    self_q,
    self_k,
    self_v,
    self_out,
    cross_q,
    cross_k,
    cross_v,
    cross_out,
    ff_gate,
    ff_up,
    ff_down,
    grad_out,
):
    core = lax.axis_index("gy")
    column = lax.axis_index("gx")
    groups = lax.axis_size("gx")
    seq_len = doc_ids.shape[1]
    half = hidden_in.shape[2]
    block = hidden_in.shape[1] // 2
    proj = self_q.shape[1]
    heads = proj // DH
    hid_part = ff_gate.shape[1]
    own_tokens = groups * block
    core_one = core.reshape(1).astype(jnp.int32)

    def to_rows(x):
        return lax.all_to_all(x, "gy", x.ndim - 2, x.ndim - 1, tiled=True)

    def to_features(x):
        return lax.all_to_all(x, "gy", x.ndim - 1, x.ndim - 2, tiled=True)

    first_rows = to_rows(hidden_in[0])
    w_self = lax.all_gather(
        jnp.concatenate([self_q, self_k, self_v], axis=1), "gy", axis=0, tiled=True
    )
    both_rows = to_rows(jnp.concatenate([encoded, grad_out], axis=0))
    w_cross = lax.all_gather(
        jnp.concatenate([cross_q, cross_k, cross_v], axis=1), "gy", axis=0, tiled=True
    )
    w_ff = lax.all_gather(jnp.concatenate([ff_gate, ff_up], axis=1), "gy", axis=0, tiled=True)
    w_outs = lax.all_gather(
        jnp.concatenate([self_out, cross_out, ff_down], axis=0), "gy", axis=1, tiled=True
    )
    w_self_out, w_cross_out, w_down = (
        w_outs[:proj],
        w_outs[proj : 2 * proj],
        w_outs[2 * proj :],
    )
    w_cq, w_ckv = w_cross[:, :proj], w_cross[:, proj:]

    twice = jnp.concatenate([buckets, buckets])

    def reversed_window(start):
        return lax.dynamic_slice_in_dim(twice, start, seq_len, 0)[::-1]

    table_part = lax.dynamic_slice_in_dim(rel_table, column * heads, heads, 1)

    def hot(near):
        return (
            near[None, :]
            == jnp.arange(rel_table.shape[0], dtype=jnp.int32)[:, None]
        ).astype(f32)

    bias_vec = lax.dot_general(
        table_part,
        hot(reversed_window(core * block + 1)),
        (((0,), (0,)), ((), ())),
        precision=lax.Precision.HIGHEST,
    )
    docs_k = doc_ids
    docs_q = lax.dynamic_index_in_dim(
        doc_ids.reshape(groups, 2, block), core, 1, keepdims=False
    ).reshape(own_tokens, 1)

    stream0 = first_rows.astype(f32)
    gains_in = [norm_gains[i : i + 1] for i in range(3)]
    (rows_one,) = boundary("first", 1, (stream0, gains_in[0]))
    qkv = mm(rows_one, w_self).astype(bf16)
    q1 = qkv[:, :proj]
    kv1 = lax.all_gather(qkv[:, proj:], "gy", axis=0)

    enc_own, rows_one = lax.optimization_barrier((both_rows[0], rows_one))
    enc_rows = gather_late(enc_own)
    kv2_own = mm(enc_rows, w_ckv).astype(bf16)
    kv2 = lax.all_gather(kv2_own, "gy", axis=0)

    ctx1 = call(
        functools.partial(self_forward_kernel, block, heads),
        jax.ShapeDtypeStruct((own_tokens, proj), bf16),
        1,
        "self_forward",
    )(core_one, q1, kv1, docs_q, docs_k, bias_vec)
    stream1, rows_two = boundary("forward", 2, (ctx1, w_self_out, stream0, gains_in[1]))
    out_own, rows_two = lax.optimization_barrier((both_rows[1], rows_two))
    out_rows = in_order(gather_late(out_own), block)
    d_hid = mm_t(out_rows, w_down)
    q2 = mm(rows_two, w_cq).astype(bf16)
    ctx2 = call(
        functools.partial(cross_forward_kernel, 2 * block, heads),
        jax.ShapeDtypeStruct((own_tokens, proj), bf16),
        0,
        "cross_forward",
    )(q2, kv2)
    stream2, rows_three = boundary("forward", 3, (ctx2, w_cross_out, stream1, gains_in[2]))
    gate_up = mm(rows_three, w_ff)
    hidden_float, glu_pull = jax.vjp(glu_piece, gate_up[:, :hid_part], gate_up[:, hid_part:])
    hid = hidden_float.astype(bf16)
    d_gate, d_up = glu_pull(d_hid)
    d_gu = jnp.concatenate([d_gate, d_up], axis=1).astype(bf16)

    def own_half(x, which):
        return lax.dynamic_slice_in_dim(x, which * half, half, 1)

    seq_rows = 16 * lax.axis_size("dp")

    def grads_of(pairs):
        def side(which):
            return jnp.concatenate(
                [t_mm(left, own_half(rows, which)) for left, rows in pairs], axis=0
            )

        total = side(core) + swap(side(1 - core).astype(bf16)).astype(f32)
        return pad_rows(total.astype(bf16), seq_rows)

    g2, gain_three, rows_a2 = boundary(
        "backward", 4, (d_gu, w_ff, stream2, gains_in[2], both_rows[1].astype(f32)), True
    )

    def slab_at(x, k):
        at = lax.rem(column + k, groups) * block
        return lax.dynamic_slice_in_dim(x, at, block, 0)

    hid_late, rows_a2 = lax.optimization_barrier((hid, rows_a2))
    layer_sum = scatter_late([mm(slab_at(hid_late, k), w_down) for k in range(groups)])
    layer_out = to_features((stream2 + layer_sum).astype(bf16))[None]
    ff_value = grads_of([(d_gu, rows_three), (hid, out_rows)])
    dctx2 = mm_t(rows_a2, w_cross_out).astype(bf16)
    dq2, dkv2_both = call(
        functools.partial(cross_backward_kernel, 2 * block, heads),
        (
            jax.ShapeDtypeStruct((own_tokens, proj), bf16),
            jax.ShapeDtypeStruct((2, 2 * proj, own_tokens), bf16),
        ),
        0,
        "cross_backward",
    )(q2, kv2, dctx2)

    def pair_sum(both):
        other = lax.dynamic_index_in_dim(both, 1 - core, 0, keepdims=False)
        own = lax.dynamic_index_in_dim(both, core, 0, keepdims=False)
        return (own.astype(f32) + swap(other).astype(f32)).astype(bf16)

    dkv2 = pair_sum(dkv2_both)
    g1, gain_two, rows_a1, ff_sum = boundary(
        "backward", 5, (dq2, w_cq, stream1, gains_in[1], g2), True, ff_value
    )
    dkv2, rows_a1 = lax.optimization_barrier((dkv2, rows_a1))
    dctx1 = mm_t(rows_a1, w_self_out).astype(bf16)
    enc_slabs = [
        lax.dot_general(
            dkv2[:, k * block : (k + 1) * block],
            w_ckv,
            (((0,), (1,)), ((), ())),
            preferred_element_type=f32,
        )
        for k in range(groups)
    ]
    grad_encoded = to_features(scatter_late(enc_slabs))[None]
    dqkv2_cross = dkv2.T
    cross_value = grads_of([(dq2, rows_two), (dqkv2_cross, enc_rows), (ctx2, rows_a2)])

    dq1, dkv1_both, by_shift = call(
        functools.partial(self_backward_kernel, block, heads),
        (
            jax.ShapeDtypeStruct((own_tokens, proj), bf16),
            jax.ShapeDtypeStruct((2, 2 * proj, own_tokens), bf16),
            jax.ShapeDtypeStruct((8, seq_len), f32),
        ),
        1,
        "self_backward",
    )(core_one, q1, kv1, docs_q, docs_k, bias_vec, dctx1)
    dkv1 = pair_sum(dkv1_both)
    dqkv1 = jnp.concatenate([dq1, dkv1.T], axis=1)
    g0, gain_one, cross_sum = boundary(
        "last", 6, (dqkv1, w_self, stream0, gains_in[0], g1), True, cross_value
    )
    grad_hidden = to_features(g0)[None]
    self_value = grads_of([(dqkv1, rows_one), (ctx1, rows_a1)])

    table_grad = lax.dot_general(
        hot(reversed_window(core * block + block)),
        by_shift[:heads],
        (((1,), (1,)), ((), ())),
        precision=lax.Precision.HIGHEST,
    )
    rel_full = lax.dynamic_update_slice(
        jnp.zeros(rel_table.shape, f32), table_grad, (0, column * heads)
    )
    flat = jnp.concatenate(
        [x.reshape(-1) for x in (gain_one, gain_two, gain_three, rel_full)]
    )
    size = flat.size
    small = pad_rows(flat.reshape(-1, 128), 8)
    self_sum, small_sum = final_sums(7, self_value, small)
    flat = small_sum.reshape(-1)[:size]
    grad_gains = flat[: norm_gains.size].reshape(norm_gains.shape)
    grad_rel = flat[norm_gains.size :].reshape(rel_table.shape)

    def turned(total, first, count):
        return total[first : first + count].T.astype(f32)

    def straight(total, first, count):
        return total[first : first + count].astype(f32)

    return (
        layer_out,
        grad_hidden,
        grad_encoded,
        grad_gains,
        grad_rel,
        turned(self_sum, 0, proj),
        turned(self_sum, proj, proj),
        turned(self_sum, 2 * proj, proj),
        straight(self_sum, 3 * proj, proj),
        turned(cross_sum, 0, proj),
        turned(cross_sum, proj, proj),
        turned(cross_sum, 2 * proj, proj),
        straight(cross_sum, 3 * proj, proj),
        turned(ff_sum, 0, hid_part),
        turned(ff_sum, hid_part, hid_part),
        straight(ff_sum, 2 * hid_part, hid_part),
    )


def solution(mesh):
    placed = (
        P("dp", "gx", "gy"),
        P("dp", "gx", "gy"),
        P("dp", None),
        P(),
        P(),
        P(),
        P("gy", "gx"),
        P("gy", "gx"),
        P("gy", "gx"),
        P("gx", "gy"),
        P("gy", "gx"),
        P("gy", "gx"),
        P("gy", "gx"),
        P("gx", "gy"),
        P("gy", "gx"),
        P("gy", "gx"),
        P("gx", "gy"),
        P("dp", "gx", "gy"),
    )
    return jax.shard_map(
        body,
        mesh=mesh,
        in_specs=placed,
        out_specs=(
            P("dp", "gx", "gy"),
            P("dp", "gx", "gy"),
            P("dp", "gx", "gy"),
            P(),
            P(),
            P("gy", "gx"),
            P("gy", "gx"),
            P("gy", "gx"),
            P("gx", "gy"),
            P("gy", "gx"),
            P("gy", "gx"),
            P("gy", "gx"),
            P("gx", "gy"),
            P("gy", "gx"),
            P("gy", "gx"),
            P("gx", "gy"),
        ),
        check_vma=False,
    )
```

```python
import functools

import jax
import jax.numpy as jnp
from jax import lax
from jax.experimental import pallas as pl
from jax.experimental.pallas import tpu as pltpu
from jax.sharding import PartitionSpec as P

DH = 64
epsilon = 1e-06
masked_score = -1000000000.0
f32 = jnp.float32
bf16 = jnp.bfloat16
VMEM_LIMIT = 48 * 1024 * 1024


def mm(a, b):
    return jnp.dot(a, b, preferred_element_type=f32)


def mm_t(a, b):
    return lax.dot_general(a, b, (((1,), (1,)), ((), ())), preferred_element_type=f32)


def t_mm(a, b):
    return lax.dot_general(a, b, (((0,), (0,)), ((), ())), preferred_element_type=f32)


def shift_gx(value, step):
    n = lax.axis_size("gx")
    return lax.ppermute(value, "gx", [(i, (i + step) % n) for i in range(n)])


def gather_late(own):
    n = lax.axis_size("gx")
    return jnp.concatenate([own] + [shift_gx(own, n - k) for k in range(1, n)], axis=0)


def in_order(cyclic, rows):
    n = lax.axis_size("gx")
    start = lax.rem(n - lax.axis_index("gx"), n) * rows
    return lax.dynamic_slice_in_dim(
        jnp.concatenate([cyclic, cyclic], axis=0), start, n * rows, 0
    )


def scatter_late(slabs):
    total = slabs[0]
    for k in range(1, len(slabs)):
        total = total + shift_gx(slabs[k].astype(bf16), k).astype(f32)
    return total


def swap(value):
    size = lax.axis_size("gy")
    return lax.ppermute(value, "gy", [(i, size - 1 - i) for i in range(size)])


def mean_last(x):
    return jnp.mean(x, axis=-1, keepdims=True)


def peer(axis, me, d, n):
    return {axis: lax.rem(me + d, n)}


def greet(axes):
    barrier = pltpu.get_barrier_semaphore()
    count = 0
    for axis, n in axes:
        me = lax.axis_index(axis)
        for d in range(1, n):
            pl.semaphore_signal(
                barrier,
                inc=1,
                device_id=peer(axis, me, d, n),
                device_id_type=pl.DeviceIdType.MESH,
            )
        count += n - 1
    pl.semaphore_wait(barrier, count)


def start_copy(source, target, send_sem, recv_sem, device):
    copy = pltpu.make_async_remote_copy(
        src_ref=source,
        dst_ref=target,
        send_sem=send_sem,
        recv_sem=recv_sem,
        device_id=device,
        device_id_type=pl.DeviceIdType.MESH,
    )
    copy.start()
    return copy


class SequenceSum:
    def __init__(self, n, value_ref, other_ref, total_ref, value, pair, got, ss, rs, ps):
        self.n, self.value, self.total, self.got = n, value, total_ref, got
        self.own, self.other, self.pair = value_ref, other_ref, pair
        self.ss, self.rs, self.ps = ss, rs, ps
        self.me = lax.axis_index("dp")
        self.rows = value_ref.shape[0] // n

    def slab(self, ref, index):
        return ref.at[pl.ds(pl.multiple_of(index * self.rows, self.rows), self.rows), :]

    def send_pair(self):
        core = lax.axis_index("gy")
        self.crossing = start_copy(
            self.other, self.pair, self.ps.at[0], self.ps.at[1], peer("gy", core, 1, 2)
        )

    def send(self):
        self.crossing.wait()
        self.value[...] = (self.own[...].astype(f32) + self.pair[...].astype(f32)).astype(bf16)
        self.copies = [
            start_copy(
                self.slab(self.value, lax.rem(self.me + d, self.n)),
                self.got.at[d],
                self.ss.at[0, d],
                self.rs.at[0, d],
                peer("dp", self.me, d, self.n),
            )
            for d in range(1, self.n)
        ]

    def add(self):
        total = self.slab(self.value, self.me)[...].astype(f32)
        for d, copy in zip(range(1, self.n), self.copies):
            copy.wait_recv()
            total = total + self.got[d].astype(f32)
        mine = self.slab(self.total, self.me)
        mine[...] = total.astype(bf16)
        self.back = [
            start_copy(
                mine, mine, self.ss.at[1, d], self.rs.at[1, d], peer("dp", self.me, d, self.n)
            )
            for d in range(1, self.n)
        ]

    def finish(self):
        for copy in self.back:
            copy.wait()
        for copy in self.copies:
            copy.wait_send()


def boundary_kernel(mode, n, seqs, transposed, *refs):
    mul = mm_t if transposed else mm
    rider = None
    if seqs:
        *refs, summed, pair, dp_got, dp_ss, dp_rs, pair_sems = refs
    if mode == "first":
        x_ref, gain_ref, rows_ref, ss, rs = refs
    elif mode == "forward":
        left_ref, w_ref, x_ref, gain_ref, out_ref, rows_ref, sent, got, ss, rs = refs
    elif mode == "backward" and not seqs:
        left_ref, w_ref, x_ref, gain_ref, g_ref, out_ref, gg_ref, rows_ref, sent, got, ss, rs = refs
    elif mode == "backward":
        (left_ref, w_ref, x_ref, gain_ref, g_ref, value_ref, other_ref) = refs[:7]
        (out_ref, gg_ref, rows_ref, total_ref, sent, got, ss, rs) = refs[7:]
    else:
        (left_ref, w_ref, x_ref, gain_ref, g_ref, value_ref, other_ref) = refs[:7]
        (out_ref, gg_ref, total_ref, sent, got, ss, rs) = refs[7:]
    me = lax.axis_index("gx")
    rows = x_ref.shape[0]
    order = sorted(range(1, n), key=lambda d: abs(2 * d - n))
    greet([("gx", n)] + ([("gy", 2), ("dp", seqs)] if seqs else []))
    if seqs:
        rider = SequenceSum(
            seqs, value_ref, other_ref, total_ref, summed, pair, dp_got, dp_ss, dp_rs, pair_sems
        )
        rider.send_pair()

    def part(column):
        at = pl.multiple_of(column * rows, rows)
        return mul(left_ref[pl.ds(at, rows), :], w_ref[...])

    copies = []
    if mode != "first":
        for d in order:
            sent[d] = part(lax.rem(me + d, n)).astype(bf16)
            copies.append(
                start_copy(sent.at[d], got.at[d], ss.at[0, d], rs.at[0, d], peer("gx", me, d, n))
            )
        total = part(me)
        if rider:
            rider.send()
        for d, copy in zip(order, copies):
            copy.wait_recv()
            total = total + got[d].astype(f32)
    gain = gain_ref[...]
    if mode in ("first", "forward"):
        stream = x_ref[...] if mode == "first" else x_ref[...] + total
        low = (stream * lax.rsqrt(mean_last(stream * stream) + epsilon) * gain).astype(bf16)
        if mode == "forward":
            out_ref[...] = stream
    else:
        stream = x_ref[...]
        root = lax.rsqrt(mean_last(stream * stream) + epsilon)
        plain = stream * root
        scaled = total * gain
        grad = g_ref[...] + root * (scaled - plain * mean_last(scaled * plain))
        gg_ref[...] = jnp.sum(total * plain, axis=0, keepdims=True)
        out_ref[...] = grad
        low = grad.astype(bf16)
    out_copies = []
    if mode != "last":
        mine = rows_ref.at[pl.ds(pl.multiple_of(me * rows, rows), rows), :]
        mine[...] = low
        out_copies = [
            start_copy(mine, mine, ss.at[1, d], rs.at[1, d], peer("gx", me, d, n)) for d in order
        ]
    if rider:
        rider.add()
    for copy in out_copies:
        copy.wait()
    for copy in copies:
        copy.wait_send()
    if rider:
        rider.finish()


def boundary(mode, cid, operands, transposed=False, value=None):
    n = lax.axis_size("gx")
    seqs = lax.axis_size("dp") if value is not None else 0
    x = operands[0 if mode == "first" else 2]
    rows, width = x.shape
    shapes = []
    if mode != "first":
        shapes.append(jax.ShapeDtypeStruct((rows, width), f32))
    if mode in ("backward", "last"):
        shapes.append(jax.ShapeDtypeStruct((1, width), f32))
    if mode != "last":
        shapes.append(jax.ShapeDtypeStruct((n * rows, width), bf16))
    scratch = []
    if mode != "first":
        scratch += [pltpu.VMEM((n, rows, width), bf16)] * 2
    scratch += [pltpu.SemaphoreType.DMA((2, n))] * 2
    if seqs:
        operands = operands + value
        value = value[0]
        shapes.append(jax.ShapeDtypeStruct(value.shape, bf16))
        scratch += [pltpu.VMEM(value.shape, bf16)] * 2
        scratch.append(pltpu.VMEM((seqs, value.shape[0] // seqs, value.shape[1]), bf16))
        scratch += [pltpu.SemaphoreType.DMA((2, seqs))] * 2
        scratch.append(pltpu.SemaphoreType.DMA((2,)))
    vm = pl.BlockSpec(memory_space=pltpu.VMEM)
    return pl.pallas_call(
        functools.partial(boundary_kernel, mode, n, seqs, transposed),
        out_shape=shapes,
        in_specs=[vm] * len(operands),
        out_specs=[vm] * len(shapes),
        scratch_shapes=scratch,
        compiler_params=pltpu.CompilerParams(
            vmem_limit_bytes=VMEM_LIMIT, collective_id=cid, has_side_effects=True
        ),
        name="boundary_" + mode,
    )(*operands)


def final_kernel(axes, small_ref, sum_ref, *scratch):
    greet(axes)
    for step, (axis, n) in enumerate(axes):
        got, ss, rs = scratch[3 * step : 3 + 3 * step]
        me = lax.axis_index(axis)
        mine = got.at[me]
        mine[...] = small_ref[...] if step == 0 else partial_sum
        copies = [
            start_copy(mine, mine, ss.at[d], rs.at[d], peer(axis, me, d, n)) for d in range(1, n)
        ]
        for copy in copies:
            copy.wait()
        partial_sum = got[0]
        for source in range(1, n):
            partial_sum = partial_sum + got[source]
    sum_ref[...] = partial_sum


def final_sums(cid, small):
    axes = [(axis, lax.axis_size(axis)) for axis in ("gy", "gx", "dp")]
    scratch = []
    for _, n in axes:
        scratch.append(pltpu.VMEM((n,) + small.shape, f32))
        scratch += [pltpu.SemaphoreType.DMA((n,))] * 2
    vm = pl.BlockSpec(memory_space=pltpu.VMEM)
    return pl.pallas_call(
        functools.partial(final_kernel, axes),
        out_shape=jax.ShapeDtypeStruct(small.shape, f32),
        in_specs=[vm],
        out_specs=vm,
        scratch_shapes=scratch,
        compiler_params=pltpu.CompilerParams(
            vmem_limit_bytes=VMEM_LIMIT, collective_id=cid, has_side_effects=True
        ),
        name="final_sums",
    )(small)


def pad_rows(value, multiple):
    return jnp.pad(value, ((0, -value.shape[0] % multiple), (0, 0)))


def natural_rows(pair_ref, width, start, block):
    pieces = []
    for b in range(2 * (width // (2 * block))):
        pieces.append(pair_ref[b % 2, (b // 2) * block : (b // 2 + 1) * block, start : start + DH])
    return jnp.concatenate(pieces, axis=0)


def softmax_rows(scores):
    top = jnp.max(scores, axis=-1, keepdims=True)
    e = jnp.exp(scores - top)
    return e * (1.0 / jnp.sum(e, axis=-1, keepdims=True))


def bias_tile(vec_ref, head, block):
    row = vec_ref[head : head + 1, :]
    return pltpu.roll(
        jnp.broadcast_to(row, (block, row.shape[1])), 0, 1, stride=1, stride_axis=0
    )


def rotate_lanes(x, amount):
    if amount == 0:
        return x
    width = x.shape[1]
    return jnp.concatenate([x[:, width - amount :], x[:, : width - amount]], axis=1)


def self_mask(core_ref, dq_ref, dk_ref, g, width, block):
    first = (2 * g + core_ref[0]) * block
    rows = first + lax.broadcasted_iota(jnp.int32, (block, width), 0)
    cols = lax.broadcasted_iota(jnp.int32, (block, width), 1)
    own = dq_ref[g * block : (g + 1) * block, :]
    return (cols <= rows) & (own == dk_ref[:, :width])


def self_scores(q, k, tile, mask, g, width, block):
    return jnp.where(mask, mm_t(q, k) + rotate_lanes(tile, 2 * block * g)[:, :width], masked_score)


def self_forward_kernel(block, heads, core_ref, q_ref, kv_ref, dq_ref, dk_ref, vec_ref, out_ref):
    groups = q_ref.shape[0] // block
    keys = 2 * q_ref.shape[0]
    masks = [
        self_mask(core_ref, dq_ref, dk_ref, g, 2 * block * (g + 1), block) for g in range(groups)
    ]
    parts = [[] for _ in range(groups)]
    for h in range(heads):
        k = natural_rows(kv_ref, keys, h * DH, block)
        v = natural_rows(kv_ref, keys, (heads + h) * DH, block)
        tile = bias_tile(vec_ref, h, block)
        for g in range(groups):
            width = 2 * block * (g + 1)
            q = q_ref[g * block : (g + 1) * block, h * DH : (h + 1) * DH]
            p = softmax_rows(self_scores(q, k[:width], tile, masks[g], g, width, block))
            parts[g].append(mm(p.astype(bf16), v[:width]))
    for g in range(groups):
        out_ref[g * block : (g + 1) * block, :] = jnp.concatenate(parts[g], axis=1).astype(bf16)


def self_backward_kernel(
    block, heads, core_ref, q_ref, kv_ref, dq_ref, dk_ref, vec_ref, dc_ref, gq_ref, gkv_ref, gd_ref
):
    groups = q_ref.shape[0] // block
    keys = 2 * q_ref.shape[0]
    masks = [
        self_mask(core_ref, dq_ref, dk_ref, g, 2 * block * (g + 1), block) for g in range(groups)
    ]
    flip = (
        lax.broadcasted_iota(jnp.int32, (block, block), 0)
        + lax.broadcasted_iota(jnp.int32, (block, block), 1)
        == block - 1
    ).astype(bf16)
    parts = [[] for _ in range(groups)]
    gd_ref[...] = jnp.zeros_like(gd_ref)
    for h in range(heads):
        k = natural_rows(kv_ref, keys, h * DH, block)
        v = natural_rows(kv_ref, keys, (heads + h) * DH, block)
        tile = bias_tile(vec_ref, h, block)
        gk_total = None
        gv_total = None
        shifted = None
        for g in range(groups - 1, -1, -1):
            width = 2 * block * (g + 1)
            q = q_ref[g * block : (g + 1) * block, h * DH : (h + 1) * DH]
            dc = dc_ref[g * block : (g + 1) * block, h * DH : (h + 1) * DH]
            p = softmax_rows(self_scores(q, k[:width], tile, masks[g], g, width, block))
            dp = mm_t(dc, v[:width])
            inner = jnp.sum(dp * p, axis=-1, keepdims=True)
            ds = (p * (dp - inner)).astype(bf16)
            parts[g].append(mm(ds, k[:width]))
            gk = t_mm(q, ds)
            gv = t_mm(dc, p.astype(bf16))
            flipped = mm(flip, ds)
            if gk_total is None:
                gk_total, gv_total = gk, gv
                shifted = rotate_lanes(flipped, keys - 2 * block * g) if g else flipped
            else:
                rest = jnp.zeros((DH, keys - width), f32)
                gk_total = gk_total + jnp.concatenate([gk, rest], axis=1)
                gv_total = gv_total + jnp.concatenate([gv, rest], axis=1)
                flipped = jnp.concatenate(
                    [flipped, jnp.zeros((block, keys - width), f32)], axis=1
                )
                if g:
                    flipped = rotate_lanes(flipped, keys - 2 * block * g)
                shifted = shifted + flipped
        for b in range(2 * groups):
            lanes = slice((b // 2) * block, (b // 2 + 1) * block)
            source = slice(b * block, (b + 1) * block)
            gkv_ref[b % 2, h * DH : (h + 1) * DH, lanes] = gk_total[:, source].astype(bf16)
            gkv_ref[b % 2, (heads + h) * DH : (heads + h + 1) * DH, lanes] = gv_total[
                :, source
            ].astype(bf16)
        gd_ref[h : h + 1, :] = jnp.sum(
            pltpu.roll(shifted, 0, 1, stride=1, stride_axis=0), axis=0, keepdims=True
        )
    for g in range(groups):
        gq_ref[g * block : (g + 1) * block, :] = jnp.concatenate(parts[g], axis=1).astype(bf16)


def cross_forward_kernel(block, heads, q_ref, kv_ref, out_ref):
    rows = q_ref.shape[0]
    for h in range(heads):
        k = jnp.concatenate([kv_ref[c, :, h * DH : (h + 1) * DH] for c in range(2)], axis=0)
        v = jnp.concatenate(
            [kv_ref[c, :, (heads + h) * DH : (heads + h + 1) * DH] for c in range(2)], axis=0
        )
        for r in range(0, rows, block):
            p = softmax_rows(mm_t(q_ref[r : r + block, h * DH : (h + 1) * DH], k))
            out_ref[r : r + block, h * DH : (h + 1) * DH] = mm(p.astype(bf16), v).astype(bf16)


def cross_backward_kernel(block, heads, q_ref, kv_ref, dc_ref, gq_ref, gkv_ref):
    rows = q_ref.shape[0]
    for h in range(heads):
        k = jnp.concatenate([kv_ref[c, :, h * DH : (h + 1) * DH] for c in range(2)], axis=0)
        v = jnp.concatenate(
            [kv_ref[c, :, (heads + h) * DH : (heads + h + 1) * DH] for c in range(2)], axis=0
        )
        gk_total = None
        for r in range(0, rows, block):
            q = q_ref[r : r + block, h * DH : (h + 1) * DH]
            dc = dc_ref[r : r + block, h * DH : (h + 1) * DH]
            p = softmax_rows(mm_t(q, k))
            dp = mm_t(dc, v)
            inner = jnp.sum(dp * p, axis=-1, keepdims=True)
            ds = (p * (dp - inner)).astype(bf16)
            gq_ref[r : r + block, h * DH : (h + 1) * DH] = mm(ds, k).astype(bf16)
            gk = t_mm(q, ds)
            gv = t_mm(dc, p.astype(bf16))
            gk_total = gk if gk_total is None else gk_total + gk
            gv_total = gv if r == 0 else gv_total + gv
        for c in range(2):
            source = slice(c * rows, (c + 1) * rows)
            gkv_ref[c, h * DH : (h + 1) * DH, :] = gk_total[:, source].astype(bf16)
            gkv_ref[c, (heads + h) * DH : (heads + h + 1) * DH, :] = gv_total[:, source].astype(
                bf16
            )


def call(kernel, out_shape, smem, name):
    vm = pl.BlockSpec(memory_space=pltpu.VMEM)

    def run(*operands):
        specs = [pl.BlockSpec(memory_space=pltpu.SMEM)] * smem + [vm] * (len(operands) - smem)
        multi = isinstance(out_shape, (list, tuple))
        return pl.pallas_call(
            kernel,
            out_shape=out_shape,
            in_specs=specs,
            out_specs=[vm] * len(out_shape) if multi else vm,
            compiler_params=pltpu.CompilerParams(vmem_limit_bytes=VMEM_LIMIT),
            name=name,
        )(*operands)

    return run


def glu_piece(gate, up_part):
    return jax.nn.gelu(gate, approximate=True) * up_part


def body(
    hidden_in,
    encoded,
    doc_ids,
    buckets,
    rel_table,
    norm_gains,
    self_q,
    self_k,
    self_v,
    self_out,
    cross_q,
    cross_k,
    cross_v,
    cross_out,
    ff_gate,
    ff_up,
    ff_down,
    grad_out,
):
    core = lax.axis_index("gy")
    column = lax.axis_index("gx")
    groups = lax.axis_size("gx")
    seq_len = doc_ids.shape[1]
    half = hidden_in.shape[2]
    block = hidden_in.shape[1] // 2
    proj = self_q.shape[1]
    heads = proj // DH
    hid_part = ff_gate.shape[1]
    own_tokens = groups * block
    core_one = core.reshape(1).astype(jnp.int32)

    def to_rows(x):
        return lax.all_to_all(x, "gy", x.ndim - 2, x.ndim - 1, tiled=True)

    def to_features(x):
        return lax.all_to_all(x, "gy", x.ndim - 1, x.ndim - 2, tiled=True)

    first_rows = to_rows(hidden_in[0])
    w_self = lax.all_gather(
        jnp.concatenate([self_q, self_k, self_v], axis=1), "gy", axis=0, tiled=True
    )
    both_rows = to_rows(jnp.concatenate([encoded, grad_out], axis=0))
    w_cross = lax.all_gather(
        jnp.concatenate([cross_q, cross_k, cross_v], axis=1), "gy", axis=0, tiled=True
    )
    w_ff = lax.all_gather(jnp.concatenate([ff_gate, ff_up], axis=1), "gy", axis=0, tiled=True)
    w_outs = lax.all_gather(
        jnp.concatenate([self_out, cross_out, ff_down], axis=0), "gy", axis=1, tiled=True
    )
    w_self_out, w_cross_out, w_down = (
        w_outs[:proj],
        w_outs[proj : 2 * proj],
        w_outs[2 * proj :],
    )
    w_cq, w_ckv = w_cross[:, :proj], w_cross[:, proj:]

    twice = jnp.concatenate([buckets, buckets])

    def reversed_window(start):
        return lax.dynamic_slice_in_dim(twice, start, seq_len, 0)[::-1]

    table_part = lax.dynamic_slice_in_dim(rel_table, column * heads, heads, 1)

    def hot(near):
        return (
            near[None, :]
            == jnp.arange(rel_table.shape[0], dtype=jnp.int32)[:, None]
        ).astype(f32)

    bias_vec = lax.dot_general(
        table_part,
        hot(reversed_window(core * block + 1)),
        (((0,), (0,)), ((), ())),
        precision=lax.Precision.HIGHEST,
    )
    docs_k = doc_ids
    docs_q = lax.dynamic_index_in_dim(
        doc_ids.reshape(groups, 2, block), core, 1, keepdims=False
    ).reshape(own_tokens, 1)

    stream0 = first_rows.astype(f32)
    gains_in = [norm_gains[i : i + 1] for i in range(3)]
    (rows_one,) = boundary("first", 1, (stream0, gains_in[0]))
    qkv = mm(rows_one, w_self).astype(bf16)
    q1 = qkv[:, :proj]
    kv1 = lax.all_gather(qkv[:, proj:], "gy", axis=0)

    enc_own, rows_one = lax.optimization_barrier((both_rows[0], rows_one))
    enc_rows = gather_late(enc_own)
    kv2_own = mm(enc_rows, w_ckv).astype(bf16)
    kv2 = lax.all_gather(kv2_own, "gy", axis=0)

    ctx1 = call(
        functools.partial(self_forward_kernel, block, heads),
        jax.ShapeDtypeStruct((own_tokens, proj), bf16),
        1,
        "self_forward",
    )(core_one, q1, kv1, docs_q, docs_k, bias_vec)
    stream1, rows_two = boundary("forward", 2, (ctx1, w_self_out, stream0, gains_in[1]))
    out_own, rows_two = lax.optimization_barrier((both_rows[1], rows_two))
    out_rows = in_order(gather_late(out_own), block)
    d_hid = mm_t(out_rows, w_down)
    q2 = mm(rows_two, w_cq).astype(bf16)
    ctx2 = call(
        functools.partial(cross_forward_kernel, 2 * block, heads),
        jax.ShapeDtypeStruct((own_tokens, proj), bf16),
        0,
        "cross_forward",
    )(q2, kv2)
    stream2, rows_three = boundary("forward", 3, (ctx2, w_cross_out, stream1, gains_in[2]))
    gate_up = mm(rows_three, w_ff)
    hidden_float, glu_pull = jax.vjp(glu_piece, gate_up[:, :hid_part], gate_up[:, hid_part:])
    hid = hidden_float.astype(bf16)
    d_gate, d_up = glu_pull(d_hid)
    d_gu = jnp.concatenate([d_gate, d_up], axis=1).astype(bf16)

    def own_half(x, which):
        return lax.dynamic_slice_in_dim(x, which * half, half, 1)

    seq_rows = 16 * lax.axis_size("dp")

    def grads_of(pairs):
        def side(which):
            return jnp.concatenate(
                [t_mm(left, own_half(rows, which)) for left, rows in pairs], axis=0
            )

        return tuple(
            pad_rows(side(which).astype(bf16), seq_rows) for which in (core, 1 - core)
        )

    ff_value = grads_of([(d_gu, rows_three), (hid, out_rows)])
    g2, gain_three, rows_a2, ff_sum = boundary(
        "backward",
        4,
        (d_gu, w_ff, stream2, gains_in[2], both_rows[1].astype(f32)),
        True,
        ff_value,
    )

    def slab_at(x, k):
        at = lax.rem(column + k, groups) * block
        return lax.dynamic_slice_in_dim(x, at, block, 0)

    hid_late, rows_a2 = lax.optimization_barrier((hid, rows_a2))
    layer_sum = scatter_late([mm(slab_at(hid_late, k), w_down) for k in range(groups)])
    layer_out = to_features((stream2 + layer_sum).astype(bf16))[None]
    dctx2 = mm_t(rows_a2, w_cross_out).astype(bf16)
    dq2, dkv2_both = call(
        functools.partial(cross_backward_kernel, 2 * block, heads),
        (
            jax.ShapeDtypeStruct((own_tokens, proj), bf16),
            jax.ShapeDtypeStruct((2, 2 * proj, own_tokens), bf16),
        ),
        0,
        "cross_backward",
    )(q2, kv2, dctx2)

    def pair_sum(both):
        other = lax.dynamic_index_in_dim(both, 1 - core, 0, keepdims=False)
        own = lax.dynamic_index_in_dim(both, core, 0, keepdims=False)
        return (own.astype(f32) + swap(other).astype(f32)).astype(bf16)

    dkv2 = pair_sum(dkv2_both)
    cross_value = grads_of([(dq2, rows_two), (dkv2.T, enc_rows), (ctx2, rows_a2)])
    g1, gain_two, rows_a1, cross_sum = boundary(
        "backward", 5, (dq2, w_cq, stream1, gains_in[1], g2), True, cross_value
    )
    dkv2, rows_a1 = lax.optimization_barrier((dkv2, rows_a1))
    dctx1 = mm_t(rows_a1, w_self_out).astype(bf16)
    enc_slabs = [
        lax.dot_general(
            dkv2[:, k * block : (k + 1) * block],
            w_ckv,
            (((0,), (1,)), ((), ())),
            preferred_element_type=f32,
        )
        for k in range(groups)
    ]
    grad_encoded = to_features(scatter_late(enc_slabs))[None]
    dq1, dkv1_both, by_shift = call(
        functools.partial(self_backward_kernel, block, heads),
        (
            jax.ShapeDtypeStruct((own_tokens, proj), bf16),
            jax.ShapeDtypeStruct((2, 2 * proj, own_tokens), bf16),
            jax.ShapeDtypeStruct((8, seq_len), f32),
        ),
        1,
        "self_backward",
    )(core_one, q1, kv1, docs_q, docs_k, bias_vec, dctx1)
    dkv1 = pair_sum(dkv1_both)
    dqkv1 = jnp.concatenate([dq1, dkv1.T], axis=1)
    self_value = grads_of([(dqkv1, rows_one), (ctx1, rows_a1)])
    g0, gain_one, self_sum = boundary(
        "last", 6, (dqkv1, w_self, stream0, gains_in[0], g1), True, self_value
    )
    grad_hidden = to_features(g0)[None]
    table_grad = lax.dot_general(
        hot(reversed_window(core * block + block)),
        by_shift[:heads],
        (((1,), (1,)), ((), ())),
        precision=lax.Precision.HIGHEST,
    )
    rel_full = lax.dynamic_update_slice(
        jnp.zeros(rel_table.shape, f32), table_grad, (0, column * heads)
    )
    flat = jnp.concatenate(
        [x.reshape(-1) for x in (gain_one, gain_two, gain_three, rel_full)]
    )
    size = flat.size
    small = pad_rows(flat.reshape(-1, 128), 8)
    small_sum = final_sums(7, small)
    flat = small_sum.reshape(-1)[:size]
    grad_gains = flat[: norm_gains.size].reshape(norm_gains.shape)
    grad_rel = flat[norm_gains.size :].reshape(rel_table.shape)

    def turned(total, first, count):
        return total[first : first + count].T.astype(f32)

    def straight(total, first, count):
        return total[first : first + count].astype(f32)

    return (
        layer_out,
        grad_hidden,
        grad_encoded,
        grad_gains,
        grad_rel,
        turned(self_sum, 0, proj),
        turned(self_sum, proj, proj),
        turned(self_sum, 2 * proj, proj),
        straight(self_sum, 3 * proj, proj),
        turned(cross_sum, 0, proj),
        turned(cross_sum, proj, proj),
        turned(cross_sum, 2 * proj, proj),
        straight(cross_sum, 3 * proj, proj),
        turned(ff_sum, 0, hid_part),
        turned(ff_sum, hid_part, hid_part),
        straight(ff_sum, 2 * hid_part, hid_part),
    )


def solution(mesh):
    placed = (
        P("dp", "gx", "gy"),
        P("dp", "gx", "gy"),
        P("dp", None),
        P(),
        P(),
        P(),
        P("gy", "gx"),
        P("gy", "gx"),
        P("gy", "gx"),
        P("gx", "gy"),
        P("gy", "gx"),
        P("gy", "gx"),
        P("gy", "gx"),
        P("gx", "gy"),
        P("gy", "gx"),
        P("gy", "gx"),
        P("gx", "gy"),
        P("dp", "gx", "gy"),
    )
    return jax.shard_map(
        body,
        mesh=mesh,
        in_specs=placed,
        out_specs=(
            P("dp", "gx", "gy"),
            P("dp", "gx", "gy"),
            P("dp", "gx", "gy"),
            P(),
            P(),
            P("gy", "gx"),
            P("gy", "gx"),
            P("gy", "gx"),
            P("gx", "gy"),
            P("gy", "gx"),
            P("gy", "gx"),
            P("gy", "gx"),
            P("gx", "gy"),
            P("gy", "gx"),
            P("gy", "gx"),
            P("gx", "gy"),
        ),
        check_vma=False,
    )
```
